512 devices in a mesh: tile: 128 (over y, z, core), lev: 4 (over x).
Axes of the slice: x: 4, y: 8, z: 8, core: 2. Of those that a mesh axis runs over, the one named last changes fastest.
Arguments:
- tracers: float32 [4, 16, 4096, 384], P(None, 'lev', 'tile'), may hold values from -6 to 6
- u_courant: float32 [16, 4096, 384], P('lev', 'tile'), may hold values from -0.3 to 0.3
- v_courant: float32 [16, 4096, 384], P('lev', 'tile'), may hold values from -0.3 to 0.3
- w_courant: float32 [16, 4096, 384], P('lev', 'tile'), may hold values from -0.3 to 0.3
- land_mask: int32 [4096, 384], P('tile'), may hold values 0 or 1
- weights: bfloat16 [8, 512, 256], replicated, may hold values from -0.078125 to 0.078125
- src_block: int32 [16384], P('tile'), may hold values from 0 to 23
- dst_tile: int32 [16384, 1], P('tile'), may hold values from 0 to 127; in each aligned block of 128 rows (0 to 127, 128 to 255, ...) at most 2 rows name the same one
- dst_block: int32 [16384], P('tile'), may hold values from 0 to 15
- pattern: int32 [16384], P('tile'), may hold values from 0 to 7
Outputs:
- new_tracers: float32 [4, 16, 4096, 384], P(None, 'lev', 'tile')
- target_fields: float32 [4, 16, 524288], P(None, 'lev', 'tile')
- target_flux: float32 [4, 16, 524288], P(None, 'lev', 'tile')
The draws below stay inside these ranges and needn't reach their ends.
Inputs may be any that keep to these rules, and one draw needn't show every extreme that they name: `dst_tile`: among the 128 entries of one strip no target strip is named more than 2 times, and some target strip is named exactly 2 times.
All inputs are finite; a program needn't handle non-finite values. No bound on the sum of `land_mask` on one device may be relied on, other than what follows from the above.
Results may differ from the reference program's by a relative error of at most 0.0041.
Values may be sent and summed in bfloat16 or wider, within the bound.
A program may use at most 128 MiB of HBM per device.

```python
import math
import jax
import jax.numpy as jnp
import numpy as np
from jax import lax

NTR = 4
CI = 32
NJ = 384
SB = 512
DB = 256
PATTERNS = 8
NBD = 16
ENT = 128
LEVELS = 16
NI = 4096
NBS = 24
NT = 524288
ENTRIES = 16384
CAP = 2
N_TILE = 128


def with_ends(result, own_key, low, largest):
    place = [jax.random.randint(jax.random.fold_in(own_key, axis), (), 0, length) for axis, length in enumerate(result.shape)]
    main_axis = result.shape.index(max(result.shape))
    next_to = place[:main_axis] + [(place[main_axis] + 1) % result.shape[main_axis]] + place[main_axis + 1:]
    return result.at[tuple(place)].set(low).at[tuple(next_to)].set(largest)


def shard_levels(rng, extent, cuts, smallest, largest):
    def one(axis_at, parts):
        heights = jax.random.uniform(jax.random.fold_in(jax.random.fold_in(rng, 6), axis_at), (parts,), jnp.float32, smallest / len(cuts), largest / len(cuts))
        return jnp.repeat(jnp.exp(heights), extent[axis_at] // parts).reshape((-1,) + (1,) * (len(extent) - axis_at - 1))

    loudness = one(*cuts[0])
    for cut in cuts[1:]:
        loudness = loudness * one(*cut)
    return loudness


def deal_out(key, own, number, rows, number_of, top, reach, lean):
    sequence = jax.random.permutation(key, number_of)
    crowded, common = portions_of(number_of, rows * top, reach, lean, True), portions_of(number_of, rows * top, reach, lean, False)
    places = jnp.arange(number_of)

    def named(lengths, turn):
        used = int((lengths > 0).sum())
        fixed = max(1, used // 4)
        shifted = fixed + (places - fixed + turn * (used - fixed)) % max(1, number_of - fixed)
        return jnp.zeros((number_of,), jnp.int32).at[sequence[jnp.where(places < fixed, places, shifted)]].set(jnp.asarray(lengths, jnp.int32))

    lengths = jnp.where(number % 4 == 0, named(crowded, number // 4), named(common, number - number // 4 - 1))
    mixed = jax.random.permutation(jax.random.fold_in(own, 3), number_of)
    donor, receiver = mixed[0:number_of // 2 * 2:2], mixed[1:number_of // 2 * 2:2]
    room = jnp.minimum(lengths[donor] - 1, reach - lengths[receiver]) // 2
    room = jnp.where((donor == sequence[0]) | (receiver == sequence[0]) | (lengths[receiver] == 0), 0, jnp.maximum(room, 0))
    shifted = jax.random.randint(jax.random.fold_in(own, 4), (number_of // 2,), 0, 1 << 20) % (room + 1)
    lengths = lengths.at[donor].add(-shifted).at[receiver].add(shifted)
    items = jnp.searchsorted(jnp.cumsum(lengths), jnp.arange(rows * top), side="right").astype(jnp.int32)
    grid = items.reshape(top, rows).T
    grid = grid[jax.random.permutation(jax.random.fold_in(own, 1), rows)]
    turn = jax.random.randint(jax.random.fold_in(own, 2), (rows, 1), 0, top)
    return jnp.take_along_axis(grid, (jnp.arange(top)[None, :] + turn) % top, axis=1)


def portions_of(amount, total, most, lean, full):
    weights = [(1 << 20) // math.isqrt(rank ** lean) + 1 for rank in range(1, amount + 1)]
    largest = most if full else min(most, max(-(-total // amount), total * weights[0] // sum(weights)))
    least = 1 if total - largest >= amount - 1 else 0
    holding, spare = [largest] + [least] * (amount - 1), total - largest - least * (amount - 1)
    while spare > 0:
        candidates = [i for i in range(1, amount) if holding[i] < largest] or [i for i in range(1, amount) if holding[i] < most]
        pool, left = sum([weights[i] for i in candidates]), spare
        for i in candidates:
            more = min(most - holding[i], max(1, left * weights[i] // pool), spare)
            holding[i] = holding[i] + more
            spare = spare - more
    return np.array(holding)


def normal_values(own_key, dims, width, reach, shards=(), kind=jnp.bfloat16):
    drawn = width * jax.random.normal(own_key, dims, jnp.float32)
    if shards:
        drawn = drawn * shard_levels(own_key, dims, shards, -0.22, 0.18)
    return jnp.clip(drawn, -reach, reach).astype(kind)


def setup_inputs(seed: int = 0) -> dict:
    splits = jax.random.split(jax.random.key(seed), 11)
    tracers = normal_values(splits[0], (NTR, LEVELS, NI, NJ), 1.0, 6.0, ((1, 4), (2, 128)), jnp.float32)
    u_courant = jnp.clip(jax.random.uniform(splits[1], (LEVELS, NI, NJ), jnp.float32, -0.3, 0.3) * shard_levels(splits[1], (LEVELS, NI, NJ), ((0, 4), (1, 128)), -0.4, 0.0), -0.3, 0.3)
    v_courant = jnp.clip(jax.random.uniform(splits[2], (LEVELS, NI, NJ), jnp.float32, -0.3, 0.3) * shard_levels(splits[2], (LEVELS, NI, NJ), ((0, 4), (1, 128)), -0.4, 0.0), -0.3, 0.3)
    w_courant = jnp.clip(jax.random.uniform(splits[3], (LEVELS, NI, NJ), jnp.float32, -0.3, 0.3) * shard_levels(splits[3], (LEVELS, NI, NJ), ((0, 4), (1, 128)), -0.4, 0.0), -0.3, 0.3)
    land_mask = with_ends((jax.random.randint(splits[4], (NI, NJ), 0, 8) < 7).astype(jnp.int32), jax.random.fold_in(splits[4], 1), 0, 1)
    weights = normal_values(splits[5], (PATTERNS, SB, DB), (12 * SB) ** -0.5, 0.078125)
    src_block = with_ends(jax.random.randint(splits[6], (ENTRIES,), 0, NBS), jax.random.fold_in(splits[6], 1), 0, NBS - 1).astype(jnp.int32)
    dst_tile_keys = jax.random.split(jax.random.fold_in(splits[7], 1), ENTRIES // ENT)
    dst_tile_turns = jax.random.permutation(jax.random.fold_in(splits[7], 3), ENTRIES // ENT)
    dst_tile = jax.vmap(lambda own, number: deal_out(jax.random.fold_in(splits[7], 2), own, number, ENT, N_TILE, 1, CAP, 2))(dst_tile_keys, dst_tile_turns).reshape((ENTRIES, 1))
    dst_block = with_ends(jax.random.randint(splits[8], (ENTRIES,), 0, NBD), jax.random.fold_in(splits[8], 1), 0, NBD - 1).astype(jnp.int32)
    pattern = with_ends(jax.random.randint(splits[9], (ENTRIES,), 0, PATTERNS), jax.random.fold_in(splits[9], 1), 0, PATTERNS - 1).astype(jnp.int32)
    return dict(tracers=tracers, u_courant=u_courant, v_courant=v_courant, w_courant=w_courant, land_mask=land_mask, weights=weights, src_block=src_block, dst_tile=dst_tile, dst_block=dst_block, pattern=pattern)


def minmod(first, second):
    return jnp.where(first * second > 0.0, jnp.sign(first) * jnp.minimum(jnp.abs(first), jnp.abs(second)), 0.0)


def face_flux(behind, left_cell, right_cell, beyond, courant, opening):
    left_slope = minmod(left_cell - behind, right_cell - left_cell)
    right_slope = minmod(right_cell - left_cell, beyond - right_cell)
    upwind = jnp.maximum(courant, 0.0) * (left_cell + 0.5 * (1.0 - courant) * left_slope)
    downwind = jnp.minimum(courant, 0.0) * (right_cell - 0.5 * (1.0 + courant) * right_slope)
    return opening * (upwind + downwind)


def reference(tracers, u_courant, v_courant, w_courant, land_mask, weights, src_block, dst_tile, dst_block, pattern):
    ocean = land_mask.astype(jnp.float32)
    east_flux = face_flux(jnp.roll(tracers, 1, 2), tracers, jnp.roll(tracers, -1, 2), jnp.roll(tracers, -2, 2),
                          u_courant, ocean * jnp.roll(ocean, -1, 0))
    west_flux = jnp.roll(east_flux, 1, 2)

    ghost_cells = jnp.flip(tracers[:, :, :, NJ - 2:], (2, 3))
    zero_row = jnp.zeros((NTR, LEVELS, NI, 1), jnp.float32)
    extended = jnp.concatenate([zero_row, tracers, ghost_cells], 3)
    mirror_courant = jnp.flip(v_courant[:, :, NJ - 1], 1)
    top_courant = 0.5 * (v_courant[:, :, NJ - 1] - mirror_courant)
    north_courant = jnp.concatenate([v_courant[:, :, :NJ - 1], top_courant[:, :, None]], 2)
    top_open = ocean[:, NJ - 1] * jnp.flip(ocean[:, NJ - 1], 0)
    north_open = jnp.concatenate([ocean[:, :NJ - 1] * ocean[:, 1:], top_open[:, None]], 1)
    north_flux = face_flux(extended[..., 0:NJ], extended[..., 1:NJ + 1], extended[..., 2:NJ + 2],
                           extended[..., 3:NJ + 3], north_courant, north_open)
    south_flux = jnp.concatenate([zero_row, north_flux[..., :NJ - 1]], 3)

    zero_levels = jnp.zeros((NTR, 2, NI, NJ), jnp.float32)
    stacked = jnp.concatenate([zero_levels, tracers, zero_levels], 1)
    level_index = jnp.arange(LEVELS, dtype=jnp.int32)
    level_open = (level_index < LEVELS - 1).astype(jnp.float32)
    below_flux = face_flux(stacked[:, 1:LEVELS + 1], stacked[:, 2:LEVELS + 2], stacked[:, 3:LEVELS + 3],
                           stacked[:, 4:LEVELS + 4], w_courant, ocean[None] * level_open[:, None, None])
    above_flux = jnp.concatenate([jnp.zeros((NTR, 1, NI, NJ), jnp.float32), below_flux[:, :LEVELS - 1]], 1)

    divergence = (east_flux - west_flux) + (north_flux - south_flux) + (below_flux - above_flux)
    new_tracers = tracers - divergence

    payload = jnp.stack([new_tracers, divergence]).astype(jnp.bfloat16)
    row_count = 2 * NTR * LEVELS
    payload_rows = payload.reshape(row_count, NI, NJ)
    owners = dst_tile[:, 0]

    def one_strip(carry, strip_index):
        strip_rows = lax.dynamic_slice_in_dim(payload_rows, (strip_index * CI).astype(jnp.int32), CI, 1)
        strip_blocks = strip_rows.reshape(row_count, NBS, SB)
        start = (strip_index * ENT).astype(jnp.int32)
        sources = lax.dynamic_slice_in_dim(src_block, start, ENT, 0)
        kind_ids = lax.dynamic_slice_in_dim(pattern, start, ENT, 0)
        owner_ids = lax.dynamic_slice_in_dim(owners, start, ENT, 0)
        block_ids = lax.dynamic_slice_in_dim(dst_block, start, ENT, 0)
        chosen = jnp.take(strip_blocks, sources, axis=1).astype(jnp.float32)
        matrices = jnp.take(weights, kind_ids, axis=0).astype(jnp.float32)
        products = jnp.einsum("rec,ecd->erd", chosen, matrices)
        rounded = lax.optimization_barrier(products.astype(jnp.bfloat16))
        slot_terms = rounded.astype(jnp.float32)
        target_ids = (owner_ids * NBD + block_ids).astype(jnp.int32)
        return carry.at[target_ids].add(slot_terms), None

    initial = jnp.zeros((N_TILE * NBD, row_count, DB), jnp.float32)
    remapped, _ = lax.scan(one_strip, initial, jnp.arange(N_TILE, dtype=jnp.int32))
    shaped = remapped.reshape(N_TILE * NBD, 2, NTR, LEVELS, DB).transpose(1, 2, 3, 0, 4)
    shaped = shaped.reshape(2, NTR, LEVELS, NT)
    return new_tracers, shaped[0], shaped[1]
```

```python
import jax
import jax.numpy as jnp
from jax import lax
from jax.experimental import pallas as pl
from jax.experimental.pallas import tpu as pltpu
from jax.sharding import PartitionSpec as P

MESH = pl.DeviceIdType.MESH
RING = 8
NBD = 16
GROUP = 16
BLOCKS = 24
SB = 512
DB = 256
PATTERNS = 8
SLOTS = 32
TARGET_ORDER = (4, 3, 5, 2, 6, 1, 7, 0)


def remap_kernel(
    x_ref, w_ref, idx_ref, dst_ref, out0, out1,
    ag, prod, terms, masks, acc, sib_out, sib_in, rs_out, rs_in,
    ag_send, ag_recv, sib_send, sib_recv, rs_send, rs_recv,
):
    me = lax.axis_index("tile")
    y, z, c = me // 16, lax.rem(me // 2, 8), lax.rem(me, 2)

    def strip(yy, zz, cc):
        return yy * 16 + zz * 2 + cc

    along_z = (strip(y, lax.rem(z + 1, RING), c), strip(y, lax.rem(z + RING - 1, RING), c))
    along_y = (strip(lax.rem(y + 1, RING), z, c), strip(lax.rem(y + RING - 1, RING), z, c))
    sibling = strip(y, z, 1 - c)
    gather_to = (along_z, along_y)
    reduce_to = (along_y, along_z)

    barrier = pltpu.get_barrier_semaphore()
    for other in (*along_z, *along_y, sibling):
        pl.semaphore_signal(barrier, inc=1, device_id={"tile": other}, device_id_type=MESH)
    pl.semaphore_wait(barrier, 5)

    half_rows = BLOCKS // 2
    streams = [(h, d) for h in range(2) for d in range(2)]
    started = []

    def gather_copy(h, d, n):
        k, sub = (n // 2 + 1, n % 2) if n < 6 else (4, d)
        rows = pl.ds(half_rows * sub, half_rows)
        src = x_ref.at[h, rows] if k == 1 else ag.at[h, d, k - 2, rows]
        dst = ag.at[h, 0 if k == 4 else d, k - 1, rows]
        return pltpu.make_async_remote_copy(
            src_ref=src, dst_ref=dst, send_sem=ag_send.at[h, d, n], recv_sem=ag_recv.at[h, d, n],
            device_id={"tile": gather_to[h][d]}, device_id_type=MESH,
        )

    def start(copy):
        copy.start()
        started.append(copy)

    for n in range(2):
        for h, d in streams:
            start(gather_copy(h, d, n))

    sub_i = lax.broadcasted_iota(jnp.int32, (NBD * GROUP, SLOTS // 2 * GROUP), 0)
    lane_i = lax.broadcasted_iota(jnp.int32, (NBD * GROUP, SLOTS // 2 * GROUP), 1)
    wanted = jnp.where(lax.rem(sub_i, GROUP) == lax.rem(lane_i, GROUP), sub_i // GROUP, -2)

    def one_mask(i, carry):
        found = dst_ref[pl.ds(i, 1), :] == wanted
        masks[i] = jnp.where(found, 1.0, 0.0).astype(jnp.bfloat16)
        return carry

    lax.fori_loop(0, 32, one_mask, 0)

    def multiply(h, j, view):
        x = view[...].reshape(BLOCKS * GROUP, SB)

        def one_pattern(p, carry):
            r = jnp.dot(x, w_ref[p], preferred_element_type=jnp.float32)
            prod[pl.ds(p * BLOCKS, BLOCKS)] = r.astype(jnp.bfloat16).reshape(BLOCKS, GROUP, DB)
            return carry

        lax.fori_loop(0, PATTERNS, one_pattern, 0)

        def one_target(t, carry):
            for r in range(2):
                i = idx_ref[(h * 8 + j) * SLOTS + t * 2 + r]
                terms[h * 16 + t, pl.ds((j * 2 + r) * GROUP, GROUP), :] = prod[i]
            return carry

        lax.fori_loop(0, 16, one_target, 0)

    def arrived(h, j):
        k, d = (j + 1) // 2, (j + 1) % 2
        multiply(h, j, ag.at[h, 0 if k == 4 else d, k - 1])

    multiply(0, 0, x_ref.at[0])
    multiply(1, 0, x_ref.at[1])
    after = {1: [(0, 1), (0, 2)], 2: [(1, 1), (1, 2)], 3: [(0, 3), (0, 4)], 4: [(1, 3), (1, 4)],
             5: [(0, 5), (0, 6), (1, 5), (1, 6)], 6: [(0, 7), (1, 7)]}
    for n in range(7):
        for h, d in streams:
            gather_copy(h, d, n).wait_recv()
            if n < 4:
                start(gather_copy(h, d, n + 2))
            elif n == 4 + d:
                start(gather_copy(h, d, 6))
        for h, j in after.get(n, ()):
            arrived(h, j)

    def sibling_copy(h, q):
        return pltpu.make_async_remote_copy(
            src_ref=sib_out.at[h, q], dst_ref=sib_in.at[h, q], send_sem=sib_send.at[h, q], recv_sem=sib_recv.at[h, q],
            device_id={"tile": sibling}, device_id_type=MESH,
        )

    def partial(q):
        for h in range(2):
            i = h * 16 + q * 2
            other = jnp.dot(masks[i + 1], terms[i + 1], preferred_element_type=jnp.float32)
            sib_out[h, q] = other.astype(jnp.bfloat16)
            start(sibling_copy(h, q))
        for h in range(2):
            i = h * 16 + q * 2
            acc[h, q] = jnp.dot(masks[i], terms[i], preferred_element_type=jnp.float32)

    def join(q):
        for h in range(2):
            sibling_copy(h, q).wait_recv()
            acc[h, q] += sib_in[h, q].astype(jnp.float32)

    half = NBD * GROUP // 2

    def reduce_copy(h, d, s, part):
        n = 0 if s == 0 else 1 + 2 * (s - 1) + part
        rows = pl.ds(part * half, half)
        return pltpu.make_async_remote_copy(
            src_ref=rs_out.at[h, d, s, rows], dst_ref=rs_in.at[h, d, s, rows],
            send_sem=rs_send.at[h, d, n], recv_sem=rs_recv.at[h, d, n],
            device_id={"tile": reduce_to[h][d]}, device_id_type=MESH,
        )

    def send_sum(h, d, s, part):
        q = 4 - s if d == 0 else 4 + s
        rows = pl.ds(part * half, half)
        rs_out[h, d, s, rows] = acc[h, q, rows].astype(jnp.bfloat16)
        start(reduce_copy(h, d, s, part))

    def take_sum(h, d, s, part):
        q = 3 - s if d == 0 else (5 + s) % 8
        rows = pl.ds(part * half, half)
        reduce_copy(h, d, s, part).wait_recv()
        acc[h, q, rows] += rs_in[h, d, s, rows].astype(jnp.float32)

    for q in (4, 3, 5):
        partial(q)
    join(4)
    for h, d in streams:
        send_sum(h, d, 0, d)
    partial(2)
    partial(6)
    join(3)
    join(5)
    for h, d in streams:
        send_sum(h, d, 1, 1 - d)
    for h, d in streams:
        take_sum(h, d, 0, d)
        send_sum(h, d, 1, d)
    for q in (1, 7, 0):
        partial(q)
    for q in (2, 6, 1, 7, 0):
        join(q)
    for s in (1, 2):
        for part in range(2):
            for h, d in streams:
                side = (1 - d, d)[part]
                take_sum(h, d, s, side)
                send_sum(h, d, s + 1, side)
    for part in range(2):
        for h, d in streams:
            take_sum(h, d, 3, (1 - d, d)[part])
    for h, out in ((0, out0), (1, out1)):
        for b in range(NBD):
            out[:, b * DB : (b + 1) * DB] = acc[h, 0, b * GROUP : (b + 1) * GROUP, :]
    for copy in started:
        copy.wait_send()


def remap(x, weights, idx, dst):
    vmem = pl.BlockSpec(memory_space=pltpu.VMEM)
    smem = pl.BlockSpec(memory_space=pltpu.SMEM)
    rows = NBD * GROUP
    bf16, f32 = jnp.bfloat16, jnp.float32
    return pl.pallas_call(
        remap_kernel,
        out_shape=[jax.ShapeDtypeStruct((GROUP, NBD * DB), f32)] * 2,
        in_specs=[vmem, vmem, smem, vmem],
        out_specs=[vmem, vmem],
        scratch_shapes=[
            pltpu.VMEM((2, 2, 4, BLOCKS, GROUP, SB), bf16),
            pltpu.VMEM((PATTERNS * BLOCKS, GROUP, DB), bf16),
            pltpu.VMEM((32, rows, DB), bf16),
            pltpu.VMEM((32, rows, DB), bf16),
            pltpu.VMEM((2, RING, rows, DB), f32),
            pltpu.VMEM((2, RING, rows, DB), bf16),
            pltpu.VMEM((2, RING, rows, DB), bf16),
            pltpu.VMEM((2, 2, 4, rows, DB), bf16),
            pltpu.VMEM((2, 2, 4, rows, DB), bf16),
            pltpu.SemaphoreType.DMA((2, 2, 7)),
            pltpu.SemaphoreType.DMA((2, 2, 7)),
            pltpu.SemaphoreType.DMA((2, RING)),
            pltpu.SemaphoreType.DMA((2, RING)),
            pltpu.SemaphoreType.DMA((2, 2, 7)),
            pltpu.SemaphoreType.DMA((2, 2, 7)),
        ],
        compiler_params=pltpu.CompilerParams(
            collective_id=1, has_side_effects=True, vmem_limit_bytes=52 * 1024 * 1024
        ),
        cost_estimate=pl.CostEstimate(flops=13_000_000_000, bytes_accessed=4_000_000, transcendentals=0),
    )(x, weights, idx, dst)


def slot_tables(src_block, dst_tile, dst_block, pattern):
    targets = dst_tile[:, 0]
    entries = targets.shape[0]
    order = jnp.arange(entries, dtype=jnp.int32)
    same = (targets[:, None] == targets[None, :]) & (order[None, :] < order[:, None])
    slot = targets * 2 + jnp.sum(same.astype(jnp.int32), 1)
    hit = slot[:, None] == jnp.arange(2 * lax.axis_size("tile"), dtype=jnp.int32)[None, :]
    values = jnp.stack([src_block, pattern, dst_block]) + 1
    return jnp.sum(jnp.where(hit[None], values[:, :, None], 0), 1) - 1


def local_tables(gathered):
    me = lax.axis_index("tile")
    y, z, c = me // 16, (me // 2) % 8, me % 2
    full = gathered.reshape(8, 8, 2, 3, 8, 8, 2, 2)
    full = lax.dynamic_index_in_dim(full, c, 2, keepdims=False)
    by_z = lax.dynamic_index_in_dim(full, y, 0, keepdims=False)
    by_z = lax.dynamic_index_in_dim(by_z, z, 3, keepdims=False)
    by_y = lax.dynamic_index_in_dim(full, z, 1, keepdims=False)
    by_y = lax.dynamic_index_in_dim(by_y, y, 2, keepdims=False)

    def turned(table, source, target):
        table = lax.dynamic_slice_in_dim(jnp.concatenate([table, table], 0), source, 8, 0)
        table = table[jnp.array([0, 7, 1, 6, 2, 5, 3, 4])]
        table = lax.dynamic_slice_in_dim(jnp.concatenate([table, table], 2), target, 8, 2)
        return jnp.where(c == 0, table, table[:, :, :, ::-1])

    both = jnp.stack([turned(by_z, z, y), turned(by_y, y, z)])
    src, pat, dst = both[:, :, 0], both[:, :, 1], both[:, :, 2]
    idx = jnp.maximum(pat * BLOCKS + src, 0).reshape(-1)
    dst = dst.transpose(0, 2, 3, 1, 4).reshape(32, 16)
    return idx, jnp.repeat(dst, GROUP, 1)


def padded(shard, sides, width, wrap):
    for axis, dim in sides:
        peers, length = (lax.axis_size(axis), shard.shape[dim])
        up = [(i, (i + 1) % peers) for i in range(peers if wrap else peers - 1)]
        down = [(j, i) for i, j in up]
        last = lax.slice_in_dim(shard, length - width, length, axis=dim)
        leading = lax.slice_in_dim(shard, 0, width, axis=dim)
        before = lax.ppermute(last, axis, up)
        after = lax.ppermute(leading, axis, down)
        shard = jnp.concatenate([before, shard, after], axis=dim)
    return shard


def minmod(first, second):
    return jnp.where(
        first * second > 0.0, jnp.sign(first) * jnp.minimum(jnp.abs(first), jnp.abs(second)), 0.0
    )


def face_flux(behind, left_cell, right_cell, beyond, courant, opening):
    left_slope = minmod(left_cell - behind, right_cell - left_cell)
    right_slope = minmod(right_cell - left_cell, beyond - right_cell)
    upwind = jnp.maximum(courant, 0.0) * (left_cell + 0.5 * (1.0 - courant) * left_slope)
    downwind = jnp.minimum(courant, 0.0) * (right_cell - 0.5 * (1.0 + courant) * right_slope)
    return opening * (upwind + downwind)


def shards(
    tracers,
    u_courant,
    v_courant,
    w_courant,
    land_mask,
    weights,
    src_block,
    dst_tile,
    dst_block,
    pattern,
):
    tracer_count, levels_dev, columns, rows_dev = tracers.shape
    ocean = land_mask.astype(jnp.float32)
    ocean_levels = jnp.broadcast_to(ocean[None, None], (1, levels_dev, columns, rows_dev))
    lateral = jnp.concatenate([tracers, ocean_levels, u_courant[None]], 0)
    widened = padded(lateral, (("tile", 2),), 2, True)
    side_cells = widened[:tracer_count]
    side_ocean = widened[tracer_count, 0]
    side_courant = widened[tracer_count + 1]
    east_faces = face_flux(
        side_cells[:, :, 0 : columns + 1],
        side_cells[:, :, 1 : columns + 2],
        side_cells[:, :, 2 : columns + 3],
        side_cells[:, :, 3 : columns + 4],
        side_courant[:, 1 : columns + 2],
        side_ocean[1 : columns + 2] * side_ocean[2 : columns + 3],
    )
    east_flux = east_faces[:, :, 1:]
    west_flux = east_faces[:, :, :columns]
    top_rows = jnp.concatenate(
        [
            tracers[..., rows_dev - 2 :],
            ocean_levels[..., rows_dev - 2 :],
            v_courant[None, :, :, rows_dev - 2 :],
        ],
        0,
    )
    strips = lax.axis_size("tile")
    partner_rows = lax.ppermute(top_rows, "tile", [(i, strips - 1 - i) for i in range(strips)])
    mirrored = jnp.flip(partner_rows, (2, 3))
    ghost_cells = mirrored[:tracer_count]
    ghost_ocean = mirrored[tracer_count, 0, :, 0]
    ghost_courant = mirrored[tracer_count + 1, :, :, 0]
    zero_row = jnp.zeros((tracer_count, levels_dev, columns, 1), jnp.float32)
    extended = jnp.concatenate([zero_row, tracers, ghost_cells], 3)
    top_courant = 0.5 * (v_courant[:, :, rows_dev - 1] - ghost_courant)
    north_courant = jnp.concatenate([v_courant[:, :, : rows_dev - 1], top_courant[:, :, None]], 2)
    top_open = ocean[:, rows_dev - 1] * ghost_ocean
    north_open = jnp.concatenate([ocean[:, : rows_dev - 1] * ocean[:, 1:], top_open[:, None]], 1)
    north_flux = face_flux(
        extended[..., 0:rows_dev],
        extended[..., 1 : rows_dev + 1],
        extended[..., 2 : rows_dev + 2],
        extended[..., 3 : rows_dev + 3],
        north_courant,
        north_open,
    )
    south_flux = jnp.concatenate([zero_row, north_flux[..., : rows_dev - 1]], 3)
    vertical = jnp.concatenate([tracers, w_courant[None]], 0)
    deepened = padded(vertical, (("lev", 1),), 2, False)
    column_cells = deepened[:tracer_count]
    column_courant = deepened[tracer_count]
    all_levels = levels_dev * lax.axis_size("lev")
    level_global = (
        lax.axis_index("lev") * levels_dev + jnp.arange(levels_dev + 1, dtype=jnp.int32) - 1
    )
    level_open = (level_global < all_levels - 1).astype(jnp.float32)
    below_faces = face_flux(
        column_cells[:, 0 : levels_dev + 1],
        column_cells[:, 1 : levels_dev + 2],
        column_cells[:, 2 : levels_dev + 3],
        column_cells[:, 3 : levels_dev + 4],
        column_courant[1 : levels_dev + 2],
        ocean[None] * level_open[:, None, None],
    )
    below_flux = below_faces[:, 1:]
    above_flux = below_faces[:, :levels_dev]
    divergence = east_flux - west_flux + (north_flux - south_flux) + (below_flux - above_flux)
    new_tracers = tracers - divergence
    payload = jnp.stack([new_tracers, divergence]).astype(jnp.bfloat16)
    blocks = payload.reshape(2, GROUP, BLOCKS, SB).transpose(0, 2, 1, 3)
    gathered = lax.all_gather(slot_tables(src_block, dst_tile, dst_block, pattern), "tile")
    idx, dst = local_tables(gathered)
    fields, fluxes = remap(blocks, weights, idx, dst)
    shape = (tracer_count, levels_dev, NBD * DB)
    return (new_tracers, fields.reshape(shape), fluxes.reshape(shape))


def solution(mesh):
    in_specs = (
        P(None, "lev", "tile", None),
        P("lev", "tile", None),
        P("lev", "tile", None),
        P("lev", "tile", None),
        P("tile", None),
        P(),
        P("tile"),
        P("tile", None),
        P("tile"),
        P("tile"),
    )
    out_specs = (P(None, "lev", "tile", None), P(None, "lev", "tile"), P(None, "lev", "tile"))
    return jax.shard_map(shards, mesh=mesh, in_specs=in_specs, out_specs=out_specs, check_vma=False)
```

```python
import jax
import jax.numpy as jnp
from jax import lax
from jax.experimental import pallas as pl
from jax.experimental.pallas import tpu as pltpu
from jax.sharding import PartitionSpec as P

MESH = pl.DeviceIdType.MESH
RING = 8
NBD = 16
GROUP = 16
BLOCKS = 24
SB = 512
DB = 256
PATTERNS = 8
SLOTS = 32
TARGET_ORDER = (4, 3, 5, 2, 6, 1, 7, 0)


def remap_kernel(
    x_ref, w_ref, tab_ref, out0, out1,
    ag, prod, terms, masks, acc, sib_out, sib_in, rs_out, rs_in,
    ag_send, ag_recv, sib_send, sib_recv, rs_send, rs_recv,
):
    me = lax.axis_index("tile")
    y, z, c = me // 16, lax.rem(me // 2, 8), lax.rem(me, 2)

    def strip(yy, zz, cc):
        return yy * 16 + zz * 2 + cc

    along_z = (strip(y, lax.rem(z + 1, RING), c), strip(y, lax.rem(z + RING - 1, RING), c))
    along_y = (strip(lax.rem(y + 1, RING), z, c), strip(lax.rem(y + RING - 1, RING), z, c))
    sibling = strip(y, z, 1 - c)
    gather_to = (along_z, along_y)
    reduce_to = (along_y, along_z)

    barrier = pltpu.get_barrier_semaphore()
    for other in (*along_z, *along_y, sibling):
        pl.semaphore_signal(barrier, inc=1, device_id={"tile": other}, device_id_type=MESH)
    pl.semaphore_wait(barrier, 5)

    half_rows = BLOCKS // 2
    streams = [(h, d) for h in range(2) for d in range(2)]
    started = []

    def gather_copy(h, d, n):
        k, sub = (n // 2 + 1, n % 2) if n < 6 else (4, d)
        rows = pl.ds(half_rows * sub, half_rows)
        src = x_ref.at[h, rows] if k == 1 else ag.at[h, d, k - 2, rows]
        dst = ag.at[h, 0 if k == 4 else d, k - 1, rows]
        return pltpu.make_async_remote_copy(
            src_ref=src, dst_ref=dst, send_sem=ag_send.at[h, d, n], recv_sem=ag_recv.at[h, d, n],
            device_id={"tile": gather_to[h][d]}, device_id_type=MESH,
        )

    def start(copy):
        copy.start()
        started.append(copy)

    for n in range(2):
        for h, d in streams:
            start(gather_copy(h, d, n))

    sub_i = lax.broadcasted_iota(jnp.int32, (NBD * GROUP, SLOTS // 2 * GROUP), 0)
    lane_i = lax.broadcasted_iota(jnp.int32, (NBD * GROUP, SLOTS // 2 * GROUP), 1)
    wanted = jnp.where(lax.rem(sub_i, GROUP) == lax.rem(lane_i, GROUP), sub_i // GROUP, -2)
    slot_of_lane = lax.broadcasted_iota(jnp.int32, (1, SLOTS // 2 * GROUP), 1) // GROUP

    def one_mask(i, carry):
        h, t = i // 16, lax.rem(i, 16)
        blocks = jnp.full((1, SLOTS // 2 * GROUP), -1, jnp.int32)
        for j in range(8):
            for r in range(2):
                blocks = jnp.where(slot_of_lane == j * 2 + r, tab_ref[h * 8 + j, 2 * SLOTS + t * 2 + r], blocks)
        masks[i] = jnp.where(blocks == wanted, 1.0, 0.0).astype(jnp.bfloat16)
        return carry

    lax.fori_loop(0, 32, one_mask, 0)

    def multiply(h, j, view):
        x = view[...].reshape(BLOCKS * GROUP, SB)

        def one_pattern(p, carry):
            r = jnp.dot(x, w_ref[p], preferred_element_type=jnp.float32)
            prod[pl.ds(p * BLOCKS, BLOCKS)] = r.astype(jnp.bfloat16).reshape(BLOCKS, GROUP, DB)
            return carry

        lax.fori_loop(0, PATTERNS, one_pattern, 0)

        def one_target(t, carry):
            for r in range(2):
                src, pat = tab_ref[h * 8 + j, t * 2 + r], tab_ref[h * 8 + j, SLOTS + t * 2 + r]
                i = jnp.clip(pat * BLOCKS + src, 0, PATTERNS * BLOCKS - 1)
                terms[h * 16 + t, pl.ds((j * 2 + r) * GROUP, GROUP), :] = prod[i]
            return carry

        lax.fori_loop(0, 16, one_target, 0)

    def arrived(h, j):
        k, d = (j + 1) // 2, (j + 1) % 2
        multiply(h, j, ag.at[h, 0 if k == 4 else d, k - 1])

    multiply(0, 0, x_ref.at[0])
    multiply(1, 0, x_ref.at[1])
    after = {1: [(0, 1), (0, 2)], 2: [(1, 1), (1, 2)], 3: [(0, 3), (0, 4)], 4: [(1, 3), (1, 4)],
             5: [(0, 5), (0, 6), (1, 5), (1, 6)], 6: [(0, 7), (1, 7)]}
    for n in range(7):
        for h, d in streams:
            gather_copy(h, d, n).wait_recv()
            if n < 4:
                start(gather_copy(h, d, n + 2))
            elif n == 4 + d:
                start(gather_copy(h, d, 6))
        for h, j in after.get(n, ()):
            arrived(h, j)

    def sibling_copy(h, q):
        return pltpu.make_async_remote_copy(
            src_ref=sib_out.at[h, q], dst_ref=sib_in.at[h, q], send_sem=sib_send.at[h, q], recv_sem=sib_recv.at[h, q],
            device_id={"tile": sibling}, device_id_type=MESH,
        )

    def partial(q):
        for h in range(2):
            i = h * 16 + q * 2
            other = jnp.dot(masks[i + 1], terms[i + 1], preferred_element_type=jnp.float32)
            sib_out[h, q] = other.astype(jnp.bfloat16)
            start(sibling_copy(h, q))
        for h in range(2):
            i = h * 16 + q * 2
            acc[h, q] = jnp.dot(masks[i], terms[i], preferred_element_type=jnp.float32)

    def join(q):
        for h in range(2):
            sibling_copy(h, q).wait_recv()
            acc[h, q] += sib_in[h, q].astype(jnp.float32)

    half = NBD * GROUP // 2

    def reduce_copy(h, d, s, part):
        n = 0 if s == 0 else 1 + 2 * (s - 1) + part
        rows = pl.ds(part * half, half)
        return pltpu.make_async_remote_copy(
            src_ref=rs_out.at[h, d, s, rows], dst_ref=rs_in.at[h, d, s, rows],
            send_sem=rs_send.at[h, d, n], recv_sem=rs_recv.at[h, d, n],
            device_id={"tile": reduce_to[h][d]}, device_id_type=MESH,
        )

    def send_sum(h, d, s, part):
        q = 4 - s if d == 0 else 4 + s
        rows = pl.ds(part * half, half)
        rs_out[h, d, s, rows] = acc[h, q, rows].astype(jnp.bfloat16)
        start(reduce_copy(h, d, s, part))

    def take_sum(h, d, s, part):
        q = 3 - s if d == 0 else (5 + s) % 8
        rows = pl.ds(part * half, half)
        reduce_copy(h, d, s, part).wait_recv()
        acc[h, q, rows] += rs_in[h, d, s, rows].astype(jnp.float32)

    for q in (4, 3, 5):
        partial(q)
    join(4)
    for h, d in streams:
        send_sum(h, d, 0, d)
    partial(2)
    partial(6)
    join(3)
    join(5)
    for h, d in streams:
        send_sum(h, d, 1, 1 - d)
    for h, d in streams:
        take_sum(h, d, 0, d)
        send_sum(h, d, 1, d)
    for q in (1, 7, 0):
        partial(q)
    for q in (2, 6, 1, 7, 0):
        join(q)
    for s in (1, 2):
        for part in range(2):
            for h, d in streams:
                side = (1 - d, d)[part]
                take_sum(h, d, s, side)
                send_sum(h, d, s + 1, side)
    for part in range(2):
        for h, d in streams:
            take_sum(h, d, 3, (1 - d, d)[part])
    for h, out in ((0, out0), (1, out1)):
        for b in range(NBD):
            out[:, b * DB : (b + 1) * DB] = acc[h, 0, b * GROUP : (b + 1) * GROUP, :]
    for copy in started:
        copy.wait_send()


def remap(x, weights, table):
    vmem = pl.BlockSpec(memory_space=pltpu.VMEM)
    smem = pl.BlockSpec(memory_space=pltpu.SMEM)
    rows = NBD * GROUP
    bf16, f32 = jnp.bfloat16, jnp.float32
    return pl.pallas_call(
        remap_kernel,
        out_shape=[jax.ShapeDtypeStruct((GROUP, NBD * DB), f32)] * 2,
        in_specs=[vmem, vmem, smem],
        out_specs=[vmem, vmem],
        scratch_shapes=[
            pltpu.VMEM((2, 2, 4, BLOCKS, GROUP, SB), bf16),
            pltpu.VMEM((PATTERNS * BLOCKS, GROUP, DB), bf16),
            pltpu.VMEM((32, rows, DB), bf16),
            pltpu.VMEM((32, rows, DB), bf16),
            pltpu.VMEM((2, RING, rows, DB), f32),
            pltpu.VMEM((2, RING, rows, DB), bf16),
            pltpu.VMEM((2, RING, rows, DB), bf16),
            pltpu.VMEM((2, 2, 4, rows, DB), bf16),
            pltpu.VMEM((2, 2, 4, rows, DB), bf16),
            pltpu.SemaphoreType.DMA((2, 2, 7)),
            pltpu.SemaphoreType.DMA((2, 2, 7)),
            pltpu.SemaphoreType.DMA((2, RING)),
            pltpu.SemaphoreType.DMA((2, RING)),
            pltpu.SemaphoreType.DMA((2, 2, 7)),
            pltpu.SemaphoreType.DMA((2, 2, 7)),
        ],
        compiler_params=pltpu.CompilerParams(
            collective_id=1, has_side_effects=True, vmem_limit_bytes=52 * 1024 * 1024
        ),
        cost_estimate=pl.CostEstimate(flops=13_000_000_000, bytes_accessed=4_000_000, transcendentals=0),
    )(x, weights, table)


def minmod(first, second):
    return jnp.maximum(jnp.minimum(first, second), jnp.minimum(jnp.maximum(first, second), 0.0))


def coefficients(courant, opening):
    up, down = jnp.maximum(courant, 0.0) * opening, jnp.minimum(courant, 0.0) * opening
    return up, up * (0.5 * (1.0 - courant)), down, down * (0.5 * (1.0 + courant))


def flux(coefs, left, left_slope, right, right_slope):
    up, up_slope, down, down_slope = coefs
    return (up * left + up_slope * left_slope) + (down * right - down_slope * right_slope)


NEAR = {1: 1, 2: 3, 3: 5, 4: 7, 5: 6, 6: 4, 7: 2}


def advect_kernel(
    tr, u_ref, v_ref, w_ref, land_ref, tab_ref, new_ref, x_ref, tab_out,
    up_out, down_out, up_in, down_in, w_in, west_tr, east_tr, west_u, west_land, east_land,
    fold_out, fold_in, mirrored, tab_in, div, staged, send, recv,
):
    tiles, levs = lax.axis_size("tile"), lax.axis_size("lev")
    me, lev = lax.axis_index("tile"), lax.axis_index("lev")
    y, z, c = me // 16, lax.rem(me // 2, 8), lax.rem(me, 2)
    ntr, nlev, cols, rows = tr.shape
    east, west = {"tile": lax.rem(me + 1, tiles)}, {"tile": lax.rem(me + tiles - 1, tiles)}
    fold = {"tile": tiles - 1 - me}
    below, above = {"lev": lax.rem(lev + 1, levs)}, {"lev": lax.rem(lev + levs - 1, levs)}
    table_to = []
    for o in range(1, 8):
        zz, yy = lax.rem(z + o, 8), lax.rem(y + o, 8)
        table_to.append((o, 0, zz, {"tile": y * 16 + zz * 2 + c}))
        table_to.append((o, 1, yy, {"tile": yy * 16 + z * 2 + c}))
    partners = [east, west, fold, below, above] + [entry[3] for entry in table_to]
    barrier = pltpu.get_barrier_semaphore()
    for other in partners:
        pl.semaphore_signal(barrier, inc=1, device_id=other, device_id_type=MESH)
    down_out[...] = tr[:, 0:2].astype(jnp.bfloat16)
    up_out[...] = tr[:, nlev - 2 : nlev].astype(jnp.bfloat16)
    lane = lax.broadcasted_iota(jnp.int32, (cols, 128), 1)
    top = rows - 128
    packed = jnp.zeros((cols, 128), jnp.float32)
    for q in range(ntr * nlev):
        tile = tr[q // nlev, q % nlev, :, top:]
        packed = jnp.where(lane == 2 * q, pltpu.roll(tile, (2 * q + 1) % 128, 1), packed)
        packed = jnp.where(lane == 2 * q + 1, pltpu.roll(tile, (2 * q + 3) % 128, 1), packed)
    first = 2 * ntr * nlev
    for k in range(nlev):
        packed = jnp.where(lane == first + k, pltpu.roll(v_ref[k, :, top:], first + k + 1, 1), packed)
    ocean = land_ref[...].astype(jnp.float32)
    packed = jnp.where(lane == first + nlev, pltpu.roll(ocean[:, top:], first + nlev + 1, 1), packed)
    fold_out[...] = packed
    pl.semaphore_wait(barrier, len(partners))

    copies = []

    def send_to(src, dst, other):
        n = len(copies)
        copies.append(pltpu.make_async_remote_copy(
            src_ref=src, dst_ref=dst, send_sem=send.at[n], recv_sem=recv.at[n], device_id=other, device_id_type=MESH,
        ))
        copies[-1].start()
        return copies[-1]

    last = cols - 8
    sent_fold = [send_to(fold_out, fold_in, fold)]
    sent_lev = [send_to(up_out, up_in, below), send_to(down_out, down_in, above), send_to(w_ref.at[nlev - 1], w_in, below)]
    sent_side = [
        send_to(tr.at[:, :, pl.ds(last, 8)], west_tr, east),
        send_to(tr.at[:, :, pl.ds(0, 8)], east_tr, west),
        send_to(u_ref.at[:, pl.ds(last, 8)], west_u, east),
        send_to(land_ref.at[pl.ds(last, 8)], west_land, east),
        send_to(land_ref.at[pl.ds(0, 8)], east_land, west),
    ]
    sent_table = [
        send_to(tab_ref.at[h * 8 + row], tab_in.at[h * 8 + NEAR[o]], other) for o, h, row, other in table_to
    ]

    for copy in sent_fold:
        copy.wait_recv()
    for i in range(cols):
        mirrored[cols - 1 - i : cols - i, :] = fold_in[i : i + 1, :]
    ghosts = mirrored[...]
    wide = rows + 128
    wide_lane = lax.broadcasted_iota(jnp.int32, (cols, rows), 1)
    nothing = jnp.zeros((cols, 128), jnp.float32)

    def ahead(a, axis):
        return pltpu.roll(a, a.shape[axis] - 1, axis)

    def behind(a, axis):
        return pltpu.roll(a, 1, axis)

    ocean_wide = jnp.concatenate(
        [ocean, jnp.where(lane == 0, pltpu.roll(ghosts, 128 - first - nlev, 1), 0.0)], 1
    )
    open_north = ocean_wide * ahead(ocean_wide, 1)
    for k in range(nlev):
        v = v_ref[k]
        other = pltpu.roll(ghosts, (127 - first - k) % 128, 1)
        fixed = jnp.where(lane == 127, 0.5 * (v[:, top:] - other), v[:, top:])
        courant = jnp.concatenate([v[:, :top], fixed, nothing], 1)
        coefs = coefficients(courant, open_north)
        for t in range(ntr):
            q = t * nlev + k
            ghost = pltpu.roll(ghosts, (128 - 2 * q) % 128, 1)
            x = jnp.concatenate([tr[t, k], jnp.where(lane < 2, ghost, 0.0)], 1)
            beyond = ahead(x, 1)
            step = beyond - x
            slope = minmod(behind(step, 1), step)
            north = flux(coefs, x, slope, beyond, ahead(slope, 1))
            div[t, k] = (north - behind(north, 1))[:, :rows]

    for copy in sent_side:
        copy.wait_recv()
    ocean_tall = jnp.concatenate(
        [west_land[...].astype(jnp.float32), ocean, east_land[...].astype(jnp.float32)], 0
    )
    open_east = ocean_tall * ahead(ocean_tall, 0)
    for k in range(nlev):
        u = u_ref[k]
        courant = jnp.concatenate([west_u[k], u, jnp.zeros((8, rows), jnp.float32)], 0)
        coefs = coefficients(courant, open_east)
        for t in range(ntr):
            x = jnp.concatenate([west_tr[t, k], tr[t, k], east_tr[t, k]], 0)
            beyond = ahead(x, 0)
            step = beyond - x
            slope = minmod(behind(step, 0), step)
            out = flux(coefs, x, slope, beyond, ahead(slope, 0))
            div[t, k] += (out - behind(out, 0))[8 : 8 + cols]

    for copy in sent_lev:
        copy.wait_recv()
    not_first = jnp.where(lev > 0, 1.0, 0.0).astype(jnp.float32)
    not_last = jnp.where(lev < levs - 1, 1.0, 0.0).astype(jnp.float32)
    for i0 in range(0, cols, 8):
        part = slice(i0, i0 + 8)
        open_part = land_ref[part, :].astype(jnp.float32)
        coefs = [coefficients(w_in[part, :], open_part * not_first)]
        for k in range(nlev):
            coefs.append(coefficients(w_ref[k, part, :], open_part * not_last if k == nlev - 1 else open_part))
        for t in range(ntr):
            cells = [up_in[t, m, part, :].astype(jnp.float32) * not_first for m in range(2)]
            cells += [tr[t, k, part, :] for k in range(nlev)]
            cells += [down_in[t, m, part, :].astype(jnp.float32) * not_last for m in range(2)]
            steps = [b - a for a, b in zip(cells[:-1], cells[1:])]
            slopes = [minmod(a, b) for a, b in zip(steps[:-1], steps[1:])]
            faces = [
                flux(coefs[f], cells[f + 1], slopes[f], cells[f + 2], slopes[f + 1]) for f in range(nlev + 1)
            ]
            for k in range(nlev):
                total = div[t, k, part, :] + (faces[k + 1] - faces[k])
                new = cells[k + 2] - total
                new_ref[t, k, part, :] = new
                q = t * nlev + k
                for kind, value in ((0, new), (1, total)):
                    for m in range(rows // 128):
                        at = (i0 * (rows // 128) + m) * GROUP + q
                        staged[kind, pl.ds(at, 8, stride=GROUP * (rows // 128)), :] = value[:, m * 128 : m * 128 + 128]

    for kind in range(2):
        for b in range(BLOCKS):
            for m in range(SB // 128):
                at = (b * (SB // 128) + m) * GROUP
                x_ref[kind, b, :, m * 128 : m * 128 + 128] = staged[kind, at : at + GROUP, :].astype(jnp.bfloat16)

    for copy in sent_table:
        copy.wait_recv()
    for h, row in ((0, z), (1, y)):
        tab_out[h * 8 : h * 8 + 1, :] = tab_ref[h * 8 + row, 0:1, :]
        for j in range(1, 8):
            tab_out[h * 8 + j : h * 8 + j + 1, :] = tab_in[h * 8 + j, 0:1, :]
    for copy in copies:
        copy.wait_send()


def advect(tracers, u, v, w, land, table):
    vmem = pl.BlockSpec(memory_space=pltpu.VMEM)
    f32, bf16 = jnp.float32, jnp.bfloat16
    ntr, nlev, cols, rows = tracers.shape
    messages = 1 + 3 + 5 + 14
    return pl.pallas_call(
        advect_kernel,
        out_shape=[
            jax.ShapeDtypeStruct(tracers.shape, f32),
            jax.ShapeDtypeStruct((2, BLOCKS, GROUP, SB), bf16),
            jax.ShapeDtypeStruct((16, 128), jnp.int32),
        ],
        in_specs=[vmem] * 6,
        out_specs=[vmem] * 3,
        scratch_shapes=[
            pltpu.VMEM((ntr, 2, cols, rows), bf16),
            pltpu.VMEM((ntr, 2, cols, rows), bf16),
            pltpu.VMEM((ntr, 2, cols, rows), bf16),
            pltpu.VMEM((ntr, 2, cols, rows), bf16),
            pltpu.VMEM((cols, rows), f32),
            pltpu.VMEM((ntr, nlev, 8, rows), f32),
            pltpu.VMEM((ntr, nlev, 8, rows), f32),
            pltpu.VMEM((nlev, 8, rows), f32),
            pltpu.VMEM((8, rows), jnp.int32),
            pltpu.VMEM((8, rows), jnp.int32),
            pltpu.VMEM((cols, 128), f32),
            pltpu.VMEM((cols, 128), f32),
            pltpu.VMEM((cols, 128), f32),
            pltpu.VMEM((16, 8, 128), jnp.int32),
            pltpu.VMEM((ntr, nlev, cols, rows), f32),
            pltpu.VMEM((2, BLOCKS * SB // 128 * GROUP, 128), f32),
            pltpu.SemaphoreType.DMA((messages,)),
            pltpu.SemaphoreType.DMA((messages,)),
        ],
        compiler_params=pltpu.CompilerParams(
            collective_id=2, has_side_effects=True, vmem_limit_bytes=32 * 1024 * 1024
        ),
        cost_estimate=pl.CostEstimate(flops=12_000_000, bytes_accessed=4_000_000, transcendentals=0),
    )(tracers, u, v, w, land, table)


def slot_tables(src_block, dst_tile, dst_block, pattern):
    me = lax.axis_index("tile")
    y, z, c = me // 16, (me // 2) % 8, me % 2
    targets = dst_tile[:, 0]
    order = jnp.arange(targets.shape[0], dtype=jnp.int32)
    same = (targets[:, None] == targets[None, :]) & (order[None, :] < order[:, None])
    rank = jnp.sum(same.astype(jnp.int32), 1)
    ty, tz, tc = targets // 16, (targets // 2) % 8, targets % 2
    low = (tc ^ c) * 2 + rank
    by_z = tz * SLOTS + ((ty - y) % 8) * 4 + low
    by_y = ty * SLOTS + ((tz - z) % 8) * 4 + low
    slot = jnp.stack([by_z, by_y])
    hit = slot[:, None, :] == jnp.arange(8 * SLOTS, dtype=jnp.int32)[None, :, None]
    values = jnp.stack([src_block, pattern, dst_block, jnp.zeros_like(pattern)]) + 1
    table = jnp.sum(jnp.where(hit[:, None], values[None, :, None, :], 0), 3) - 1
    table = table.reshape(2, 4, 8, SLOTS).transpose(0, 2, 1, 3).reshape(16, 1, 128)
    return jnp.broadcast_to(table, (16, 8, 128))


def shards(
    tracers,
    u_courant,
    v_courant,
    w_courant,
    land_mask,
    weights,
    src_block,
    dst_tile,
    dst_block,
    pattern,
):
    table = slot_tables(src_block, dst_tile, dst_block, pattern)
    new_tracers, payload, tables = advect(tracers, u_courant, v_courant, w_courant, land_mask, table)
    fields, fluxes = remap(payload, weights, tables)
    shape = tracers.shape[:2] + (NBD * DB,)
    return (new_tracers, fields.reshape(shape), fluxes.reshape(shape))


def solution(mesh):
    in_specs = (
        P(None, "lev", "tile", None),
        P("lev", "tile", None),
        P("lev", "tile", None),
        P("lev", "tile", None),
        P("tile", None),
        P(),
        P("tile"),
        P("tile", None),
        P("tile"),
        P("tile"),
    )
    out_specs = (P(None, "lev", "tile", None), P(None, "lev", "tile"), P(None, "lev", "tile"))
    return jax.shard_map(shards, mesh=mesh, in_specs=in_specs, out_specs=out_specs, check_vma=False)
```

```python
import jax
import jax.numpy as jnp
from jax import lax
from jax.experimental import pallas as pl
from jax.experimental.pallas import tpu as pltpu
from jax.sharding import PartitionSpec as P

MESH = pl.DeviceIdType.MESH
RING = 8
NBD = 16
GROUP = 16
BLOCKS = 24
SB = 512
DB = 256
PATTERNS = 8
SLOTS = 32
PARTS = 4
HALVES = (range(0, PARTS // 2), range(PARTS // 2, PARTS))


def minmod(first, second):
    return jnp.maximum(jnp.minimum(first, second), jnp.minimum(jnp.maximum(first, second), 0.0))


def coefficients(courant, opening):
    up, down = jnp.maximum(courant, 0.0) * opening, jnp.minimum(courant, 0.0) * opening
    return up, up * (0.5 * (1.0 - courant)), down, down * (0.5 * (1.0 + courant))


def flux(coefs, left, left_slope, right, right_slope):
    up, up_slope, down, down_slope = coefs
    return (up * left + up_slope * left_slope) + (down * right - down_slope * right_slope)


NEAR = {1: 1, 2: 3, 3: 5, 4: 7, 5: 6, 6: 4, 7: 2}


def slot_tables(tab_src, y, z, c, src_ref, tile_ref, block_ref, pattern_ref):
    entries = tile_ref.shape[1]
    targets = tile_ref[...]
    square = (entries, entries)
    row_i = lax.broadcasted_iota(jnp.int32, square, 0)
    lane_i = lax.broadcasted_iota(jnp.int32, square, 1)
    as_rows = jnp.broadcast_to(targets.astype(jnp.float32), square)
    same = jnp.where((jnp.transpose(as_rows) == as_rows) & (row_i < lane_i), 1.0, 0.0)
    rank = jnp.sum(same, axis=0, keepdims=True).astype(jnp.int32)
    ty, tz, tc = targets >> 4, (targets >> 1) & 7, targets & 1
    low = jnp.bitwise_xor(tc, c) * 2 + rank
    value, slot_i = row_i // SLOTS, lax.rem(row_i, SLOTS)
    named = jnp.where(value == 0, src_ref[...] + 1, jnp.where(value == 1, pattern_ref[...] + 1, block_ref[...] + 1))
    named = jnp.where(value == 3, 0, named).astype(jnp.float32)
    place_i = lax.broadcasted_iota(jnp.int32, (16, entries), 0)
    for h, place, slot in ((0, tz, ((ty - y) & 7) * 4 + low), (1, ty, ((tz - z) & 7) * 4 + low)):
        filled = jnp.where(slot == slot_i, named, 0.0).astype(jnp.bfloat16)
        chosen = jnp.where(place == place_i, 1.0, 0.0).astype(jnp.bfloat16)
        table = lax.dot_general(chosen, filled, (((1,), (1,)), ((), ())), preferred_element_type=jnp.float32)
        table = table.astype(jnp.int32) - 1
        for p in range(8):
            tab_src[h * 8 + p] = jnp.broadcast_to(table[p : p + 1, :], (8, 128))


def kernel(
    tr_hbm, u_hbm, v_hbm, w_hbm, land_hbm, weights_hbm, src_ref, tile_ref, block_ref, pattern_ref,
    new_ref, out0, out1,
    tr, u_ref, v_ref, w_ref, land_ref, weights,
    up_out, down_out, up_in, down_in, w_in, west_tr, east_tr, west_u, west_land, east_land,
    fold_out, fold_in, mirrored, tab_src, tab_in, tab, tab_s, div, staged,
    x_ref, ag, prod, terms, terms_out, masks, acc, rs_out, rs_in,
    load, send, recv, ag_send, ag_recv, sib_send, sib_recv, rs_send, rs_recv,
):
    tiles, levs = lax.axis_size("tile"), lax.axis_size("lev")
    me, lev = lax.axis_index("tile"), lax.axis_index("lev")
    y, z, c = me // 16, lax.rem(me // 2, 8), lax.rem(me, 2)
    ntr, nlev, cols, rows = tr.shape

    def strip(yy, zz, cc):
        return {"tile": yy * 16 + zz * 2 + cc}

    east, west = {"tile": lax.rem(me + 1, tiles)}, {"tile": lax.rem(me + tiles - 1, tiles)}
    fold = {"tile": tiles - 1 - me}
    below, above = {"lev": lax.rem(lev + 1, levs)}, {"lev": lax.rem(lev + levs - 1, levs)}
    sibling = strip(y, z, 1 - c)
    table_to = []
    for o in range(1, 8):
        zz, yy = lax.rem(z + o, 8), lax.rem(y + o, 8)
        table_to.append((o, 0, zz, strip(y, zz, c)))
        table_to.append((o, 1, yy, strip(yy, z, c)))
    partners = [east, west, fold, below, above] + [entry[3] for entry in table_to]
    along_z = (strip(y, lax.rem(z + 1, RING), c), strip(y, lax.rem(z + RING - 1, RING), c))
    along_y = (strip(lax.rem(y + 1, RING), z, c), strip(lax.rem(y + RING - 1, RING), z, c))
    gather_to = (along_z, along_y)
    reduce_to = (along_y, along_z)

    barrier = pltpu.get_barrier_semaphore()
    for other in partners:
        pl.semaphore_signal(barrier, inc=1, device_id=other, device_id_type=MESH)
    loads = [
        pltpu.make_async_copy(src, dst, load.at[n])
        for n, (src, dst) in enumerate((
            (tr_hbm, tr), (land_hbm, land_ref), (v_hbm, v_ref), (u_hbm, u_ref), (w_hbm, w_ref), (weights_hbm, weights)
        ))
    ]
    for copy in loads[:5]:
        copy.start()
    slot_tables(tab_src, y, z, c, src_ref, tile_ref, block_ref, pattern_ref)
    loads[0].wait()
    down_out[...] = tr[:, 0:2].astype(jnp.bfloat16)
    up_out[...] = tr[:, nlev - 2 : nlev].astype(jnp.bfloat16)
    for n in range(1, 5):
        loads[n].wait()
    lane = lax.broadcasted_iota(jnp.int32, (cols, 128), 1)
    top = rows - 128
    packed = jnp.zeros((cols, 128), jnp.float32)
    for q in range(ntr * nlev):
        tile = tr[q // nlev, q % nlev, :, top:]
        packed = jnp.where(lane == 2 * q, pltpu.roll(tile, (2 * q + 1) % 128, 1), packed)
        packed = jnp.where(lane == 2 * q + 1, pltpu.roll(tile, (2 * q + 3) % 128, 1), packed)
    first = 2 * ntr * nlev
    for k in range(nlev):
        packed = jnp.where(lane == first + k, pltpu.roll(v_ref[k, :, top:], first + k + 1, 1), packed)
    ocean = land_ref[...].astype(jnp.float32)
    packed = jnp.where(lane == first + nlev, pltpu.roll(ocean[:, top:], first + nlev + 1, 1), packed)
    fold_out[...] = packed
    pl.semaphore_wait(barrier, len(partners))

    copies = []
    started = []

    def start(copy):
        copy.start()
        started.append(copy)

    def send_to(src, dst, other):
        n = len(copies)
        copies.append(pltpu.make_async_remote_copy(
            src_ref=src, dst_ref=dst, send_sem=send.at[n], recv_sem=recv.at[n], device_id=other, device_id_type=MESH,
        ))
        start(copies[-1])
        return copies[-1]

    last, middle = cols - 8, cols // 2
    sent_fold = [send_to(fold_out, fold_in, fold)]
    sent_side = [
        send_to(tr.at[:, :, pl.ds(last, 8)], west_tr, east),
        send_to(tr.at[:, :, pl.ds(0, 8)], east_tr, west),
        send_to(u_ref.at[:, pl.ds(last, 8)], west_u, east),
        send_to(land_ref.at[pl.ds(last, 8)], west_land, east),
        send_to(land_ref.at[pl.ds(0, 8)], east_land, west),
    ]
    sent_lev = []
    for at in (pl.ds(0, middle), pl.ds(middle, middle)):
        sent_lev.append([
            send_to(up_out.at[:, :, at], up_in.at[:, :, at], below),
            send_to(down_out.at[:, :, at], down_in.at[:, :, at], above),
            send_to(w_ref.at[nlev - 1, at], w_in.at[at], below),
        ])
    sent_table = [
        send_to(tab_src.at[h * 8 + row], tab_in.at[h * 8 + NEAR[o]], other) for o, h, row, other in table_to
    ]

    loads[5].start()

    def ahead(a, axis):
        return pltpu.roll(a, a.shape[axis] - 1, axis)

    def behind(a, axis):
        return pltpu.roll(a, 1, axis)

    for copy in sent_side:
        copy.wait_recv()
    ocean_tall = jnp.concatenate(
        [west_land[...].astype(jnp.float32), ocean, east_land[...].astype(jnp.float32)], 0
    )
    open_east = ocean_tall * ahead(ocean_tall, 0)
    for k in range(nlev):
        courant = jnp.concatenate([west_u[k], u_ref[k], jnp.zeros((8, rows), jnp.float32)], 0)
        coefs = coefficients(courant, open_east)
        for t in range(ntr):
            x = jnp.concatenate([west_tr[t, k], tr[t, k], east_tr[t, k]], 0)
            beyond = ahead(x, 0)
            step = beyond - x
            slope = minmod(behind(step, 0), step)
            out = flux(coefs, x, slope, beyond, ahead(slope, 0))
            div[t, k] = (out - behind(out, 0))[8 : 8 + cols]

    for copy in sent_table:
        copy.wait_recv()
    for h, row in ((0, z), (1, y)):
        tab[h * 8 : h * 8 + 1, :] = tab_src[h * 8 + row, 0:1, :]
        for j in range(1, 8):
            tab[h * 8 + j : h * 8 + j + 1, :] = tab_in[h * 8 + j, 0:1, :]
    sent_tables = send_to(tab.at[pl.ds(0, 16)], tab.at[pl.ds(16, 16)], sibling)

    for copy in sent_fold:
        copy.wait_recv()
    for i in range(cols):
        mirrored[cols - 1 - i : cols - i, :] = fold_in[i : i + 1, :]
    ghosts = mirrored[...]
    nothing = jnp.zeros((cols, 128), jnp.float32)
    ocean_wide = jnp.concatenate(
        [ocean, jnp.where(lane == 0, pltpu.roll(ghosts, 128 - first - nlev, 1), 0.0)], 1
    )
    open_north = ocean_wide * ahead(ocean_wide, 1)

    def north_part(part):
        for k in range(nlev):
            v = v_ref[k, part, :]
            other = pltpu.roll(ghosts[part], (127 - first - k) % 128, 1)
            fixed = jnp.where(lane[part] == 127, 0.5 * (v[:, top:] - other), v[:, top:])
            courant = jnp.concatenate([v[:, :top], fixed, nothing[part]], 1)
            coefs = coefficients(courant, open_north[part])
            for t in range(ntr):
                ghost = pltpu.roll(ghosts[part], (128 - 2 * (t * nlev + k)) % 128, 1)
                x = jnp.concatenate([tr[t, k, part, :], jnp.where(lane[part] < 2, ghost, 0.0)], 1)
                beyond = ahead(x, 1)
                step = beyond - x
                slope = minmod(behind(step, 1), step)
                north = flux(coefs, x, slope, beyond, ahead(slope, 1))
                div[t, k, part, :] += (north - behind(north, 1))[:, :rows]

    streams = [(h, d) for h in range(2) for d in range(2)]
    quarter = BLOCKS // 4

    def gather_copy(h, d, n):
        k, sub = (n // 4 + 1, n % 4) if n < 12 else (4, 2 * d + n - 12)
        blocks = pl.ds(quarter * sub, quarter)
        src = x_ref.at[h, blocks] if k == 1 else ag.at[h, d, k - 2, blocks]
        dst = ag.at[h, 0 if k == 4 else d, k - 1, blocks]
        return pltpu.make_async_remote_copy(
            src_ref=src, dst_ref=dst, send_sem=ag_send.at[h, d, n], recv_sem=ag_recv.at[h, d, n],
            device_id=gather_to[h][d], device_id_type=MESH,
        )

    not_first = jnp.where(lev > 0, 1.0, 0.0).astype(jnp.float32)
    not_last = jnp.where(lev < levs - 1, 1.0, 0.0).astype(jnp.float32)
    across = rows // 128
    for i0 in range(0, cols, 8):
        part = slice(i0, i0 + 8)
        north_part(part)
        if i0 % middle == 0:
            for copy in sent_lev[i0 // middle]:
                copy.wait_recv()
        open_part = land_ref[part, :].astype(jnp.float32)
        coefs = [coefficients(w_in[part, :], open_part * not_first)]
        for k in range(nlev):
            coefs.append(coefficients(w_ref[k, part, :], open_part * not_last if k == nlev - 1 else open_part))
        for t in range(ntr):
            cells = [up_in[t, m, part, :].astype(jnp.float32) * not_first for m in range(2)]
            cells += [tr[t, k, part, :] for k in range(nlev)]
            cells += [down_in[t, m, part, :].astype(jnp.float32) * not_last for m in range(2)]
            steps = [b - a for a, b in zip(cells[:-1], cells[1:])]
            slopes = [minmod(a, b) for a, b in zip(steps[:-1], steps[1:])]
            faces = [
                flux(coefs[f], cells[f + 1], slopes[f], cells[f + 2], slopes[f + 1]) for f in range(nlev + 1)
            ]
            for k in range(nlev):
                total = div[t, k, part, :] + (faces[k + 1] - faces[k])
                new = cells[k + 2] - total
                new_ref[t, k, part, :] = new
                q = t * nlev + k
                for kind, value in ((0, new), (1, total)):
                    for m in range(across):
                        at = (i0 * across + m) * GROUP + q
                        staged[kind, pl.ds(at, 8, stride=GROUP * across), :] = value[:, m * 128 : m * 128 + 128]
        for kind in range(2):
            for b in range(i0 * rows // SB, (i0 + 8) * rows // SB):
                for m in range(SB // 128):
                    at = (b * (SB // 128) + m) * GROUP
                    x_ref[kind, b, :, m * 128 : m * 128 + 128] = staged[kind, at : at + GROUP, :].astype(jnp.bfloat16)
        for h, d in streams:
            start(gather_copy(h, d, i0 // 8))

    sent_tables.wait_recv()
    to_scalars = pltpu.make_async_copy(tab, tab_s, load.at[6])
    to_scalars.start()
    to_scalars.wait()
    lanes = 2 * 8 * 2 * GROUP
    sub_i = lax.broadcasted_iota(jnp.int32, (NBD * GROUP, lanes), 0)
    lane_i = lax.broadcasted_iota(jnp.int32, (NBD * GROUP, lanes), 1)
    wanted = jnp.where(lax.rem(sub_i, GROUP) == lax.rem(lane_i, GROUP), sub_i // GROUP, -2)
    slot_of_lane = lax.broadcasted_iota(jnp.int32, (1, lanes), 1) // GROUP

    def one_mask(i, carry):
        h, q = i // 8, lax.rem(i, 8)
        blocks = jnp.full((1, lanes), -1, jnp.int32)
        for core in range(2):
            for j in range(8):
                for r in range(2):
                    named = tab_s[core * 16 + h * 8 + j, 2 * SLOTS + q * 4 + core * 2 + r]
                    blocks = jnp.where(slot_of_lane == (core * 8 + j) * 2 + r, named, blocks)
        masks[i] = jnp.where(blocks == wanted, 1.0, 0.0).astype(jnp.bfloat16)
        return carry

    lax.fori_loop(0, 16, one_mask, 0)
    loads[5].wait()

    def sibling_copy(h, j):
        at = pl.ds((8 + j) * 2 * GROUP, 2 * GROUP)
        return pltpu.make_async_remote_copy(
            src_ref=terms_out.at[h, j], dst_ref=terms.at[pl.ds(h * 8, 8), at],
            send_sem=sib_send.at[h, j], recv_sem=sib_recv.at[h, j], device_id=sibling, device_id_type=MESH,
        )

    def multiply(view, b0, count):
        x = view[b0 : b0 + count].reshape(count * GROUP, SB)

        def one_pattern(p, carry):
            r = jnp.dot(x, weights[p], preferred_element_type=jnp.float32)
            prod[pl.ds(p * BLOCKS + b0, count)] = r.astype(jnp.bfloat16).reshape(count, GROUP, DB)
            return carry

        lax.fori_loop(0, PATTERNS, one_pattern, 0, unroll=PATTERNS)

    def pick(h, j):
        def product(slot):
            src, pat = tab_s[h * 8 + j, slot], tab_s[h * 8 + j, SLOTS + slot]
            return prod[jnp.clip(pat * BLOCKS + src, 0, PATTERNS * BLOCKS - 1)]

        def one_target(q, carry):
            for r in range(2):
                terms_out[h, j, q, r * GROUP : (r + 1) * GROUP, :] = product(q * 4 + 2 + r)
            for r in range(2):
                at = (j * 2 + r) * GROUP
                terms[h * 8 + q, at : at + GROUP, :] = product(q * 4 + r)
            return carry

        lax.fori_loop(0, 8, one_target, 0, unroll=4)
        start(sibling_copy(h, j))

    def arrived(h, j):
        k, d = (j + 1) // 2, (j + 1) % 2
        multiply(x_ref.at[h] if j == 0 else ag.at[h, d, k - 1], 0, BLOCKS)
        pick(h, j)

    waiting = [(0, 0), (1, 0)]
    for n in range(12):
        for h, d in streams:
            gather_copy(h, d, n).wait_recv()
            if n < 8:
                start(gather_copy(h, d, n + 4))
            elif (n - 8) // 2 == d:
                start(gather_copy(h, d, 12 + (n - 8) % 2))
        if waiting:
            arrived(*waiting.pop(0))
        if n % 4 == 3:
            k = n // 4 + 1
            waiting += [(0, 2 * k - 1), (0, 2 * k), (1, 2 * k - 1), (1, 2 * k)]
    while waiting:
        arrived(*waiting.pop(0))
    for h in range(2):
        for n in (12, 13):
            for d in range(2):
                gather_copy(h, d, n).wait_recv()
        multiply(ag.at[h, 0, 3], 0, BLOCKS)
        pick(h, 7)

    size = NBD * GROUP // PARTS

    def partial(h, *targets):
        for q in targets:
            acc[h, q] = jnp.dot(masks[h * 8 + q], terms[h * 8 + q], preferred_element_type=jnp.float32)

    def reduce_copy(h, d, s, part):
        at = pl.ds(part * size, size)
        n = PARTS * s + part
        return pltpu.make_async_remote_copy(
            src_ref=rs_out.at[h, d, s, at], dst_ref=rs_in.at[h, d, s, at],
            send_sem=rs_send.at[h, d, n], recv_sem=rs_recv.at[h, d, n],
            device_id=reduce_to[h][d], device_id_type=MESH,
        )

    def came(h, d, s, part, at):
        reduce_copy(h, d, s, part).wait_recv()
        return rs_in[h, d, s, at].astype(jnp.float32)

    def pass_on(h, d, s, part):
        at = pl.ds(part * size, size)
        total = acc[h, 4 - s if d == 0 else 4 + s, at]
        if s > 1 or (s == 1 and part in HALVES[d]):
            total += came(h, d, s - 1, part, at)
        rs_out[h, d, s, at] = total.astype(jnp.bfloat16)
        start(reduce_copy(h, d, s, part))

    order = [[*HALVES[1 - d], *HALVES[d]] for d in range(2)]
    for h in range(2):
        for j in range(8):
            sibling_copy(h, j).wait_recv()
        partial(h, 4)
        for p in range(PARTS // 2):
            for d in range(2):
                pass_on(h, d, 0, HALVES[d][p])
    for h in range(2):
        partial(h, 3, 5)
        for p in range(PARTS // 2):
            for d in range(2):
                pass_on(h, d, 1, order[d][p])
    for h in range(2):
        partial(h, 2, 6)
    for p in range(PARTS // 2, PARTS):
        for h, d in streams:
            pass_on(h, d, 1, order[d][p])
    for h in range(2):
        partial(h, 1, 7)
    for p in range(PARTS):
        for h, d in streams:
            pass_on(h, d, 2, order[d][p])
    for h in range(2):
        partial(h, 0)
    for p in range(PARTS):
        for h, d in streams:
            pass_on(h, d, 3, order[d][p])
    for p in range(PARTS):
        for h, out in ((0, out0), (1, out1)):
            part = order[0][p]
            at = pl.ds(part * size, size)
            total = acc[h, 0, at] + came(h, 0, 3, part, at) + came(h, 1, 3, part, at)
            for i in range(size // GROUP):
                b = part * (size // GROUP) + i
                for t in range(ntr):
                    at_row = i * GROUP + t * nlev
                    out[t, :, b * DB : (b + 1) * DB] = total[at_row : at_row + nlev]
    for copy in started:
        copy.wait_send()


def deliver(new_in, fields_in, fluxes_in, new_out, fields_out, fluxes_out, done):
    pairs = ((new_in, new_out), (fields_in, fields_out), (fluxes_in, fluxes_out))
    copies = [pltpu.make_async_copy(src, dst, done.at[n]) for n, (src, dst) in enumerate(pairs)]
    for copy in copies:
        copy.start()
    for copy in copies:
        copy.wait()


def shards(
    tracers,
    u_courant,
    v_courant,
    w_courant,
    land_mask,
    weights,
    src_block,
    dst_tile,
    dst_block,
    pattern,
):
    vmem = pl.BlockSpec(memory_space=pltpu.VMEM)
    anywhere = pl.BlockSpec(memory_space=pl.ANY)
    f32, bf16, i32 = jnp.float32, jnp.bfloat16, jnp.int32
    ntr, nlev, cols, rows = tracers.shape
    height = NBD * GROUP
    dma = pltpu.SemaphoreType.DMA
    messages = 1 + 5 + 6 + 14 + 1
    new_tracers, fields, fluxes = pl.pallas_call(
        kernel,
        out_shape=[
            jax.ShapeDtypeStruct(tracers.shape, f32),
            jax.ShapeDtypeStruct((ntr, nlev, NBD * DB), f32),
            jax.ShapeDtypeStruct((ntr, nlev, NBD * DB), f32),
        ],
        in_specs=[anywhere] * 6 + [vmem] * 4,
        out_specs=[vmem] * 3,
        scratch_shapes=[
            pltpu.VMEM(tracers.shape, f32),
            pltpu.VMEM((nlev, cols, rows), f32),
            pltpu.VMEM((nlev, cols, rows), f32),
            pltpu.VMEM((nlev, cols, rows), f32),
            pltpu.VMEM((cols, rows), i32),
            pltpu.VMEM(weights.shape, bf16),
            pltpu.VMEM((ntr, 2, cols, rows), bf16),
            pltpu.VMEM((ntr, 2, cols, rows), bf16),
            pltpu.VMEM((ntr, 2, cols, rows), bf16),
            pltpu.VMEM((ntr, 2, cols, rows), bf16),
            pltpu.VMEM((cols, rows), f32),
            pltpu.VMEM((ntr, nlev, 8, rows), f32),
            pltpu.VMEM((ntr, nlev, 8, rows), f32),
            pltpu.VMEM((nlev, 8, rows), f32),
            pltpu.VMEM((8, rows), i32),
            pltpu.VMEM((8, rows), i32),
            pltpu.VMEM((cols, 128), f32),
            pltpu.VMEM((cols, 128), f32),
            pltpu.VMEM((cols, 128), f32),
            pltpu.VMEM((16, 8, 128), i32),
            pltpu.VMEM((16, 8, 128), i32),
            pltpu.VMEM((32, 128), i32),
            pltpu.SMEM((32, 128), i32),
            pltpu.VMEM(tracers.shape, f32),
            pltpu.VMEM((2, BLOCKS * SB // 128 * GROUP, 128), f32),
            pltpu.VMEM((2, BLOCKS, GROUP, SB), bf16),
            pltpu.VMEM((2, 2, 4, BLOCKS, GROUP, SB), bf16),
            pltpu.VMEM((PATTERNS * BLOCKS, GROUP, DB), bf16),
            pltpu.VMEM((16, 32 * GROUP, DB), bf16),
            pltpu.VMEM((2, 8, 8, 2 * GROUP, DB), bf16),
            pltpu.VMEM((16, height, 32 * GROUP), bf16),
            pltpu.VMEM((2, RING, height, DB), f32),
            pltpu.VMEM((2, 2, 4, height, DB), bf16),
            pltpu.VMEM((2, 2, 4, height, DB), bf16),
            dma((7,)),
            dma((messages,)),
            dma((messages,)),
            dma((2, 2, 14)),
            dma((2, 2, 14)),
            dma((2, 8)),
            dma((2, 8)),
            dma((2, 2, 4 * PARTS)),
            dma((2, 2, 4 * PARTS)),
        ],
        compiler_params=pltpu.CompilerParams(
            collective_id=1, has_side_effects=True, vmem_limit_bytes=54 * 1024 * 1024
        ),
        cost_estimate=pl.CostEstimate(flops=14_000_000_000, bytes_accessed=6_000_000, transcendentals=0),
    )(
        tracers, u_courant, v_courant, w_courant, land_mask, weights,
        *(a.reshape(1, -1) for a in (src_block, dst_tile, dst_block, pattern)),
    )
    results = (new_tracers, fields, fluxes)
    return tuple(pl.pallas_call(
        deliver,
        out_shape=[jax.ShapeDtypeStruct(a.shape, a.dtype) for a in results],
        in_specs=[vmem] * 3,
        out_specs=[anywhere] * 3,
        scratch_shapes=[dma((3,))],
    )(*results))


def solution(mesh):
    in_specs = (
        P(None, "lev", "tile", None),
        P("lev", "tile", None),
        P("lev", "tile", None),
        P("lev", "tile", None),
        P("tile", None),
        P(),
        P("tile"),
        P("tile", None),
        P("tile"),
        P("tile"),
    )
    out_specs = (P(None, "lev", "tile", None), P(None, "lev", "tile"), P(None, "lev", "tile"))
    return jax.shard_map(shards, mesh=mesh, in_specs=in_specs, out_specs=out_specs, check_vma=False)
```

```python
import jax
import jax.numpy as jnp
from jax import lax
from jax.experimental import pallas as pl
from jax.experimental.pallas import tpu as pltpu
from jax.sharding import PartitionSpec as P

MESH = pl.DeviceIdType.MESH
RING = 8
NBD = 16
GROUP = 16
BLOCKS = 24
SB = 512
DB = 256
PATTERNS = 8
SLOTS = 32
QUARTERS = (1, 2, 0, 3)
PARTS = 4
HALVES = (range(0, PARTS // 2), range(PARTS // 2, PARTS))


def minmod(first, second):
    return jnp.maximum(jnp.minimum(first, second), jnp.minimum(jnp.maximum(first, second), 0.0))


def coefficients(courant, opening):
    up, down = jnp.maximum(courant, 0.0) * opening, jnp.minimum(courant, 0.0) * opening
    return up, up * (0.5 * (1.0 - courant)), down, down * (0.5 * (1.0 + courant))


def flux(coefs, left, left_slope, right, right_slope):
    up, up_slope, down, down_slope = coefs
    return (up * left + up_slope * left_slope) + (down * right - down_slope * right_slope)


NEAR = {1: 1, 2: 3, 3: 5, 4: 7, 5: 6, 6: 4, 7: 2}


def slot_tables(tab_src, y, z, c, src_ref, tile_ref, block_ref, pattern_ref):
    entries = tile_ref.shape[1]
    targets = tile_ref[...]
    square = (entries, entries)
    row_i = lax.broadcasted_iota(jnp.int32, square, 0)
    lane_i = lax.broadcasted_iota(jnp.int32, square, 1)
    as_rows = jnp.broadcast_to(targets.astype(jnp.float32), square)
    same = jnp.where((jnp.transpose(as_rows) == as_rows) & (row_i < lane_i), 1.0, 0.0)
    rank = jnp.sum(same, axis=0, keepdims=True).astype(jnp.int32)
    ty, tz, tc = targets >> 4, (targets >> 1) & 7, targets & 1
    low = jnp.bitwise_xor(tc, c) * 2 + rank
    value, slot_i = row_i // SLOTS, lax.rem(row_i, SLOTS)
    named = jnp.where(value == 0, src_ref[...] + 1, jnp.where(value == 1, pattern_ref[...] + 1, block_ref[...] + 1))
    named = jnp.where(value == 3, 0, named).astype(jnp.float32)
    place_i = lax.broadcasted_iota(jnp.int32, (16, entries), 0)
    for h, place, slot in ((0, tz, ((ty - y) & 7) * 4 + low), (1, ty, ((tz - z) & 7) * 4 + low)):
        filled = jnp.where(slot == slot_i, named, 0.0).astype(jnp.bfloat16)
        chosen = jnp.where(place == place_i, 1.0, 0.0).astype(jnp.bfloat16)
        table = lax.dot_general(chosen, filled, (((1,), (1,)), ((), ())), preferred_element_type=jnp.float32)
        table = table.astype(jnp.int32) - 1
        for p in range(8):
            tab_src[h * 8 + p] = jnp.broadcast_to(table[p : p + 1, :], (8, 128))


def kernel(
    tr_hbm, u_hbm, v_hbm, w_hbm, land_hbm, weights_hbm, src_ref, tile_ref, block_ref, pattern_ref,
    new_hbm, out0, out1,
    tr, u_ref, v_ref, w_ref, land_ref, weights,
    up_out, down_out, up_in, down_in, w_in, east_out, west_out, west_in, east_in,
    fold_out, fold_in, mirrored, tab_src, tab_in, tab, tab_s, div, staged, new_ref,
    x_ref, ag, prod, terms, terms_out, masks, acc, rs_out, rs_in,
    load, send, recv, ag_send, ag_recv, sib_send, sib_recv, rs_send, rs_recv,
):
    tiles, levs = lax.axis_size("tile"), lax.axis_size("lev")
    me, lev = lax.axis_index("tile"), lax.axis_index("lev")
    y, z, c = me // 16, lax.rem(me // 2, 8), lax.rem(me, 2)
    ntr, nlev, cols, rows = tr.shape

    def strip(yy, zz, cc):
        return {"tile": yy * 16 + zz * 2 + cc}

    east, west = {"tile": lax.rem(me + 1, tiles)}, {"tile": lax.rem(me + tiles - 1, tiles)}
    fold = {"tile": tiles - 1 - me}
    below, above = {"lev": lax.rem(lev + 1, levs)}, {"lev": lax.rem(lev + levs - 1, levs)}
    sibling = strip(y, z, 1 - c)
    table_to = []
    for o in range(1, 8):
        zz, yy = lax.rem(z + o, 8), lax.rem(y + o, 8)
        table_to.append((o, 0, zz, strip(y, zz, c)))
        table_to.append((o, 1, yy, strip(yy, z, c)))
    partners = [east, west, fold, below, above] + [entry[3] for entry in table_to]
    along_z = (strip(y, lax.rem(z + 1, RING), c), strip(y, lax.rem(z + RING - 1, RING), c))
    along_y = (strip(lax.rem(y + 1, RING), z, c), strip(lax.rem(y + RING - 1, RING), z, c))
    gather_to = (along_z, along_y)
    reduce_to = (along_y, along_z)

    barrier = pltpu.get_barrier_semaphore()
    for other in partners:
        pl.semaphore_signal(barrier, inc=1, device_id=other, device_id_type=MESH)
    loads = [
        pltpu.make_async_copy(src, dst, load.at[n])
        for n, (src, dst) in enumerate((
            (tr_hbm, tr), (land_hbm, land_ref), (v_hbm, v_ref), (u_hbm, u_ref), (w_hbm, w_ref), (weights_hbm, weights)
        ))
    ]
    for copy in loads[:5]:
        copy.start()
    slot_tables(tab_src, y, z, c, src_ref, tile_ref, block_ref, pattern_ref)
    for n in range(5):
        loads[n].wait()
    lane = lax.broadcasted_iota(jnp.int32, (cols, 128), 1)
    top = rows - 128
    packed = jnp.zeros((cols, 128), jnp.float32)
    for q in range(ntr * nlev):
        tile = tr[q // nlev, q % nlev, :, top:]
        packed = jnp.where(lane == 2 * q, pltpu.roll(tile, (2 * q + 1) % 128, 1), packed)
        packed = jnp.where(lane == 2 * q + 1, pltpu.roll(tile, (2 * q + 3) % 128, 1), packed)
    first = 2 * ntr * nlev
    for k in range(nlev):
        packed = jnp.where(lane == first + k, pltpu.roll(v_ref[k, :, top:], first + k + 1, 1), packed)
    ocean = land_ref[...].astype(jnp.float32)
    packed = jnp.where(lane == first + nlev, pltpu.roll(ocean[:, top:], first + nlev + 1, 1), packed)
    fold_out[...] = packed
    last = cols - 8
    east_out[first : first + 8, :] = jnp.zeros((8, rows), jnp.float32)
    west_out[first : first + 8, :] = jnp.zeros((8, rows), jnp.float32)
    for q in range(ntr * nlev):
        east_out[2 * q : 2 * q + 2, :] = tr[q // nlev, q % nlev, cols - 2 : cols, :]
        west_out[2 * q : 2 * q + 2, :] = tr[q // nlev, q % nlev, 0:2, :]
    for k in range(nlev):
        east_out[first + k : first + k + 1, :] = u_ref[k, cols - 1 : cols, :]
    east_out[first + nlev : first + nlev + 1, :] = ocean[cols - 1 : cols]
    west_out[first + nlev : first + nlev + 1, :] = ocean[0:1]
    for n in QUARTERS:
        for t in range(ntr):
            for out, k in ((down_out, 0), (up_out, nlev - 2)):
                two = [tr[t, k + m, n * 8 : n * 8 + 8, :] for m in range(2)]
                out[n, t * 16 : t * 16 + 16, :] = jnp.concatenate(two, 0).astype(jnp.bfloat16)
    pl.semaphore_wait(barrier, len(partners))

    copies = []
    started = []

    def start(copy):
        copy.start()
        started.append(copy)

    def send_to(src, dst, other):
        n = len(copies)
        copies.append(pltpu.make_async_remote_copy(
            src_ref=src, dst_ref=dst, send_sem=send.at[n], recv_sem=recv.at[n], device_id=other, device_id_type=MESH,
        ))
        start(copies[-1])
        return copies[-1]

    sent_fold = [send_to(fold_out, fold_in, fold)]

    def send_levels(n):
        at = pl.ds(n * 8, 8)
        return [
            send_to(up_out.at[n], up_in.at[n], below),
            send_to(down_out.at[n], down_in.at[n], above),
            send_to(w_ref.at[nlev - 1, at], w_in.at[at], below),
        ]

    sent_lev = {QUARTERS[0]: send_levels(QUARTERS[0])}
    sent_side = [send_to(east_out, west_in, east), send_to(west_out, east_in, west)]
    for n in QUARTERS[1:]:
        sent_lev[n] = send_levels(n)
    sent_table = [
        send_to(tab_src.at[h * 8 + row], tab_in.at[h * 8 + NEAR[o]], other) for o, h, row, other in table_to
    ]

    loads[5].start()

    def ahead(a, axis):
        return pltpu.roll(a, a.shape[axis] - 1, axis)

    def behind(a, axis):
        return pltpu.roll(a, 1, axis)

    def east_part(cells, courants, mask, columns, at):
        opening = mask * ahead(mask, 0)
        for k in range(nlev):
            coefs = coefficients(courants(k), opening)
            for t in range(ntr):
                x = cells(t, k)
                beyond = ahead(x, 0)
                step = beyond - x
                slope = minmod(behind(step, 0), step)
                out = flux(coefs, x, slope, beyond, ahead(slope, 0))
                div[t, k, columns, :] = (out - behind(out, 0))[at]

    inner = slice(8, cols - 8)
    east_part(lambda t, k: tr[t, k], lambda k: u_ref[k], ocean, inner, inner)

    def unpacked(packed_ref, row, at):
        tile = packed_ref[row // 8 * 8 : row // 8 * 8 + 8, :]
        turn = (at - row) % 8
        return pltpu.roll(tile, turn, 0) if turn else tile

    def east_ends(n):
        if n == 0:
            mask = jnp.concatenate([unpacked(west_in, first + nlev, 7), ocean[:16]], 0)
            east_part(
                lambda t, k: jnp.concatenate([unpacked(west_in, 2 * (t * nlev + k), 6), tr[t, k, :16, :]], 0),
                lambda k: jnp.concatenate([unpacked(west_in, first + k, 7), u_ref[k, :16, :]], 0),
                mask, slice(0, 8), slice(8, 16),
            )
        else:
            mask = jnp.concatenate([ocean[cols - 16 :], unpacked(east_in, first + nlev, 0)], 0)
            east_part(
                lambda t, k: jnp.concatenate([tr[t, k, cols - 16 :, :], unpacked(east_in, 2 * (t * nlev + k), 0)], 0),
                lambda k: jnp.concatenate([u_ref[k, cols - 16 :, :], jnp.zeros((8, rows), jnp.float32)], 0),
                mask, slice(last, cols), slice(8, 16),
            )

    for copy in sent_fold:
        copy.wait_recv()
    for i in range(cols):
        mirrored[cols - 1 - i : cols - i, :] = fold_in[i : i + 1, :]
    ghosts = mirrored[...]
    nothing = jnp.zeros((cols, 128), jnp.float32)
    ocean_wide = jnp.concatenate(
        [ocean, jnp.where(lane == 0, pltpu.roll(ghosts, 128 - first - nlev, 1), 0.0)], 1
    )
    open_north = ocean_wide * ahead(ocean_wide, 1)

    def north_part(part):
        for k in range(nlev):
            v = v_ref[k, part, :]
            other = pltpu.roll(ghosts[part], (127 - first - k) % 128, 1)
            fixed = jnp.where(lane[part] == 127, 0.5 * (v[:, top:] - other), v[:, top:])
            courant = jnp.concatenate([v[:, :top], fixed, nothing[part]], 1)
            coefs = coefficients(courant, open_north[part])
            for t in range(ntr):
                ghost = pltpu.roll(ghosts[part], (128 - 2 * (t * nlev + k)) % 128, 1)
                x = jnp.concatenate([tr[t, k, part, :], jnp.where(lane[part] < 2, ghost, 0.0)], 1)
                beyond = ahead(x, 1)
                step = beyond - x
                slope = minmod(behind(step, 1), step)
                north = flux(coefs, x, slope, beyond, ahead(slope, 1))
                div[t, k, part, :] += (north - behind(north, 1))[:, :rows]

    streams = [(h, d) for h in range(2) for d in range(2)]
    quarter = BLOCKS // 4

    def gather_copy(h, d, n):
        k, at = (n // 4 + 1, n % 4) if n < 12 else (4, 2 * (n - 12) + d)
        blocks = pl.ds(quarter * at, quarter)
        src = x_ref.at[h, pl.ds(quarter * QUARTERS[at], quarter)] if k == 1 else ag.at[h, d, k - 2, blocks]
        dst = ag.at[h, 0 if k == 4 else d, k - 1, blocks]
        return pltpu.make_async_remote_copy(
            src_ref=src, dst_ref=dst, send_sem=ag_send.at[h, d, n], recv_sem=ag_recv.at[h, d, n],
            device_id=gather_to[h][d], device_id_type=MESH,
        )

    not_first = jnp.where(lev > 0, 1.0, 0.0).astype(jnp.float32)
    not_last = jnp.where(lev < levs - 1, 1.0, 0.0).astype(jnp.float32)
    across = rows // 128
    for turn, quarter_at in enumerate(QUARTERS):
        i0 = quarter_at * 8
        part = slice(i0, i0 + 8)
        if turn == 2:
            for copy in sent_side:
                copy.wait_recv()
        if turn >= 2:
            east_ends(quarter_at)
        north_part(part)
        for copy in sent_lev[quarter_at]:
            copy.wait_recv()
        open_part = land_ref[part, :].astype(jnp.float32)
        coefs = [coefficients(w_in[part, :], open_part * not_first)]
        for k in range(nlev):
            coefs.append(coefficients(w_ref[k, part, :], open_part * not_last if k == nlev - 1 else open_part))
        for t in range(ntr):
            beneath, over = (a[quarter_at, t * 16 : t * 16 + 16, :].astype(jnp.float32) for a in (down_in, up_in))
            cells = [over[:8] * not_first, over[8:] * not_first]
            cells += [tr[t, k, part, :] for k in range(nlev)]
            cells += [beneath[:8] * not_last, beneath[8:] * not_last]
            steps = [b - a for a, b in zip(cells[:-1], cells[1:])]
            slopes = [minmod(a, b) for a, b in zip(steps[:-1], steps[1:])]
            faces = [
                flux(coefs[f], cells[f + 1], slopes[f], cells[f + 2], slopes[f + 1]) for f in range(nlev + 1)
            ]
            for k in range(nlev):
                total = div[t, k, part, :] + (faces[k + 1] - faces[k])
                new = cells[k + 2] - total
                new_ref[t, k, part, :] = new
                q = t * nlev + k
                for kind, value in ((0, new), (1, total)):
                    for m in range(across):
                        at = (i0 * across + m) * GROUP + q
                        staged[kind, pl.ds(at, 8, stride=GROUP * across), :] = value[:, m * 128 : m * 128 + 128]
        for kind in range(2):
            for b in range(i0 * rows // SB, (i0 + 8) * rows // SB):
                for m in range(SB // 128):
                    at = (b * (SB // 128) + m) * GROUP
                    x_ref[kind, b, :, m * 128 : m * 128 + 128] = staged[kind, at : at + GROUP, :].astype(jnp.bfloat16)
        for h, d in streams:
            start(gather_copy(h, d, turn))
    new_copy = pltpu.make_async_copy(new_ref, new_hbm, load.at[7])
    new_copy.start()

    lanes = 2 * 8 * 2 * GROUP
    sub_i = lax.broadcasted_iota(jnp.int32, (NBD * GROUP, lanes), 0)
    lane_i = lax.broadcasted_iota(jnp.int32, (NBD * GROUP, lanes), 1)
    wanted = jnp.where(lax.rem(sub_i, GROUP) == lax.rem(lane_i, GROUP), sub_i // GROUP, -2)
    slot_of_lane = lax.broadcasted_iota(jnp.int32, (1, lanes), 1) // GROUP

    def one_mask(i, carry):
        h, q = i // 8, lax.rem(i, 8)
        blocks = jnp.full((1, lanes), -1, jnp.int32)
        for core in range(2):
            for j in range(8):
                for r in range(2):
                    named = tab_s[core * 16 + h * 8 + j, 2 * SLOTS + q * 4 + core * 2 + r]
                    blocks = jnp.where(slot_of_lane == (core * 8 + j) * 2 + r, named, blocks)
        masks[i] = jnp.where(blocks == wanted, 1.0, 0.0).astype(jnp.bfloat16)
        return carry


    def sibling_copy(h, j):
        at = pl.ds((8 + j) * 2 * GROUP, 2 * GROUP)
        return pltpu.make_async_remote_copy(
            src_ref=terms_out.at[h, j], dst_ref=terms.at[pl.ds(h * 8, 8), at],
            send_sem=sib_send.at[h, j], recv_sem=sib_recv.at[h, j], device_id=sibling, device_id_type=MESH,
        )

    def multiply(at, view, first_quarter, places):
        count = quarter * len(places)
        x = view[quarter * first_quarter : quarter * first_quarter + count].reshape(count * GROUP, SB)

        def one_pattern(p, carry):
            r = jnp.dot(x, weights[p], preferred_element_type=jnp.float32)
            r = r.astype(jnp.bfloat16).reshape(count, GROUP, DB)
            for i, place in enumerate(places):
                prod[at, pl.ds(p * BLOCKS + quarter * place, quarter)] = r[i * quarter : (i + 1) * quarter]
            return carry

        lax.fori_loop(0, PATTERNS, one_pattern, 0, unroll=PATTERNS)

    def pick(h, j, at):
        def product(slot):
            src, pat = tab_s[h * 8 + j, slot], tab_s[h * 8 + j, SLOTS + slot]
            return prod[at, jnp.clip(pat * BLOCKS + src, 0, PATTERNS * BLOCKS - 1)]

        def one_target(q, carry):
            for r in range(2):
                terms_out[h, j, q, r * GROUP : (r + 1) * GROUP, :] = product(q * 4 + 2 + r)
            for r in range(2):
                at = (j * 2 + r) * GROUP
                terms[h * 8 + q, at : at + GROUP, :] = product(q * 4 + r)
            return carry

        lax.fori_loop(0, 8, one_target, 0, unroll=4)
        start(sibling_copy(h, j))

    def own(h):
        multiply(h * 2, x_ref.at[h], 0, range(4))
        pick(h, 0, h * 2)

    def whole(k, h, d):
        multiply(h * 2 + d, ag.at[h, d, k - 1], 0, QUARTERS)
        pick(h, 2 * k - 1 + d, h * 2 + d)

    def early(k, h, d):
        multiply(h * 2 + d, ag.at[h, d, k - 1], 0, QUARTERS[:2])

    def late(k, h, d):
        multiply(h * 2 + d, ag.at[h, d, k - 1], 2, QUARTERS[2:])
        pick(h, 2 * k - 1 + d, h * 2 + d)

    waiting = [(own, 0), (own, 1)]
    todo = {3: (whole, 1), 5: (early, 2), 7: (late, 2), 9: (early, 3), 11: (late, 3)}
    for n in range(12):
        for h, d in streams:
            gather_copy(h, d, n).wait_recv()
            if n < 8:
                start(gather_copy(h, d, n + 4))
            elif n % 2 == d:
                start(gather_copy(h, d, 12 + (n - 8) // 2))
        if n == 0:
            for copy in sent_table:
                copy.wait_recv()
            for h, row in ((0, z), (1, y)):
                tab[h * 8 : h * 8 + 1, :] = tab_src[h * 8 + row, 0:1, :]
                for j in range(1, 8):
                    tab[h * 8 + j : h * 8 + j + 1, :] = tab_in[h * 8 + j, 0:1, :]
            sent_tables = send_to(tab.at[pl.ds(0, 16)], tab.at[pl.ds(16, 16)], sibling)

        elif n == 1:
            sent_tables.wait_recv()
            to_scalars = pltpu.make_async_copy(tab, tab_s, load.at[6])
            to_scalars.start()
            to_scalars.wait()
            lax.fori_loop(0, 16, one_mask, 0)
            loads[5].wait()
        for _ in range(2 if n > 1 else 0):
            if waiting:
                work, *of = waiting.pop(0)
                work(*of)
        if n in todo:
            waiting += [(*todo[n], h, d) for h, d in streams]
    for work, *of in waiting:
        work(*of)
    for n, work in ((12, early), (13, late)):
        for h in range(2):
            for d in range(2):
                gather_copy(h, d, n).wait_recv()
            work(4, h, 0)

    size = NBD * GROUP // PARTS

    def partial(h, *targets):
        for q in targets:
            acc[h, q] = jnp.dot(masks[h * 8 + q], terms[h * 8 + q], preferred_element_type=jnp.float32)

    def reduce_copy(h, d, s, part):
        at = pl.ds(part * size, size)
        n = PARTS * s + part
        return pltpu.make_async_remote_copy(
            src_ref=rs_out.at[h, d, s, at], dst_ref=rs_in.at[h, d, s, at],
            send_sem=rs_send.at[h, d, n], recv_sem=rs_recv.at[h, d, n],
            device_id=reduce_to[h][d], device_id_type=MESH,
        )

    def came(h, d, s, part, at):
        reduce_copy(h, d, s, part).wait_recv()
        return rs_in[h, d, s, at].astype(jnp.float32)

    def pass_on(h, d, s, part):
        at = pl.ds(part * size, size)
        total = acc[h, 4 - s if d == 0 else 4 + s, at]
        if s > 1 or (s == 1 and part in HALVES[d]):
            total += came(h, d, s - 1, part, at)
        rs_out[h, d, s, at] = total.astype(jnp.bfloat16)
        start(reduce_copy(h, d, s, part))

    order = [[*HALVES[1 - d], *HALVES[d]] for d in range(2)]
    for h in range(2):
        for j in range(8):
            sibling_copy(h, j).wait_recv()
        partial(h, 4)
        for p in range(PARTS // 2):
            for d in range(2):
                pass_on(h, d, 0, HALVES[d][p])
    for h in range(2):
        partial(h, 3, 5)
        for p in range(PARTS // 2):
            for d in range(2):
                pass_on(h, d, 1, order[d][p])
    for h in range(2):
        partial(h, 2, 6)
    for p in range(PARTS // 2, PARTS):
        for h, d in streams:
            pass_on(h, d, 1, order[d][p])
    for h in range(2):
        partial(h, 1, 7)
    for p in range(PARTS):
        for h, d in streams:
            pass_on(h, d, 2, order[d][p])
    for h in range(2):
        partial(h, 0)
    for p in range(PARTS):
        for h, d in streams:
            pass_on(h, d, 3, order[d][p])
    for p in range(PARTS):
        for h, out in ((0, out0), (1, out1)):
            part = order[0][p]
            at = pl.ds(part * size, size)
            total = acc[h, 0, at] + came(h, 0, 3, part, at) + came(h, 1, 3, part, at)
            for i in range(size // GROUP):
                b = part * (size // GROUP) + i
                for t in range(ntr):
                    at_row = i * GROUP + t * nlev
                    out[t, :, b * DB : (b + 1) * DB] = total[at_row : at_row + nlev]
    new_copy.wait()
    for copy in started:
        copy.wait_send()


def deliver(new_in, fields_in, fluxes_in, new_out, fields_out, fluxes_out, new, fields, fluxes, load, store):
    pieces = [(fields_in, fields, fields_out), (fluxes_in, fluxes, fluxes_out)]
    pieces += [(new_in.at[t], new.at[t], new_out.at[t]) for t in range(new.shape[0])]
    loads = [pltpu.make_async_copy(src, held, load.at[n]) for n, (src, held, _) in enumerate(pieces)]
    stores = [pltpu.make_async_copy(held, dst, store.at[n]) for n, (_, held, dst) in enumerate(pieces)]
    for copy in loads:
        copy.start()
    for arriving, leaving in zip(loads, stores):
        arriving.wait()
        leaving.start()
    for copy in stores:
        copy.wait()


def shards(
    tracers,
    u_courant,
    v_courant,
    w_courant,
    land_mask,
    weights,
    src_block,
    dst_tile,
    dst_block,
    pattern,
):
    vmem = pl.BlockSpec(memory_space=pltpu.VMEM)
    anywhere = pl.BlockSpec(memory_space=pl.ANY)
    f32, bf16, i32 = jnp.float32, jnp.bfloat16, jnp.int32
    ntr, nlev, cols, rows = tracers.shape
    height = NBD * GROUP
    dma = pltpu.SemaphoreType.DMA
    messages = 1 + 2 + 12 + 14 + 1
    new_tracers, fields, fluxes = pl.pallas_call(
        kernel,
        out_shape=[
            jax.ShapeDtypeStruct(tracers.shape, f32),
            jax.ShapeDtypeStruct((ntr, nlev, NBD * DB), f32),
            jax.ShapeDtypeStruct((ntr, nlev, NBD * DB), f32),
        ],
        in_specs=[anywhere] * 6 + [vmem] * 4,
        out_specs=[anywhere, vmem, vmem],
        scratch_shapes=[
            pltpu.VMEM(tracers.shape, f32),
            pltpu.VMEM((nlev, cols, rows), f32),
            pltpu.VMEM((nlev, cols, rows), f32),
            pltpu.VMEM((nlev, cols, rows), f32),
            pltpu.VMEM((cols, rows), i32),
            pltpu.VMEM(weights.shape, bf16),
            pltpu.VMEM((4, ntr * 16, rows), bf16),
            pltpu.VMEM((4, ntr * 16, rows), bf16),
            pltpu.VMEM((4, ntr * 16, rows), bf16),
            pltpu.VMEM((4, ntr * 16, rows), bf16),
            pltpu.VMEM((cols, rows), f32),
            pltpu.VMEM((2 * ntr * nlev + 8, rows), f32),
            pltpu.VMEM((2 * ntr * nlev + 8, rows), f32),
            pltpu.VMEM((2 * ntr * nlev + 8, rows), f32),
            pltpu.VMEM((2 * ntr * nlev + 8, rows), f32),
            pltpu.VMEM((cols, 128), f32),
            pltpu.VMEM((cols, 128), f32),
            pltpu.VMEM((cols, 128), f32),
            pltpu.VMEM((16, 8, 128), i32),
            pltpu.VMEM((16, 8, 128), i32),
            pltpu.VMEM((32, 128), i32),
            pltpu.SMEM((32, 128), i32),
            pltpu.VMEM(tracers.shape, f32),
            pltpu.VMEM((2, BLOCKS * SB // 128 * GROUP, 128), f32),
            pltpu.VMEM(tracers.shape, f32),
            pltpu.VMEM((2, BLOCKS, GROUP, SB), bf16),
            pltpu.VMEM((2, 2, 4, BLOCKS, GROUP, SB), bf16),
            pltpu.VMEM((4, PATTERNS * BLOCKS, GROUP, DB), bf16),
            pltpu.VMEM((16, 32 * GROUP, DB), bf16),
            pltpu.VMEM((2, 8, 8, 2 * GROUP, DB), bf16),
            pltpu.VMEM((16, height, 32 * GROUP), bf16),
            pltpu.VMEM((2, RING, height, DB), f32),
            pltpu.VMEM((2, 2, 4, height, DB), bf16),
            pltpu.VMEM((2, 2, 4, height, DB), bf16),
            dma((8,)),
            dma((messages,)),
            dma((messages,)),
            dma((2, 2, 14)),
            dma((2, 2, 14)),
            dma((2, 8)),
            dma((2, 8)),
            dma((2, 2, 4 * PARTS)),
            dma((2, 2, 4 * PARTS)),
        ],
        compiler_params=pltpu.CompilerParams(
            collective_id=1, has_side_effects=True, vmem_limit_bytes=54 * 1024 * 1024
        ),
        cost_estimate=pl.CostEstimate(flops=14_000_000_000, bytes_accessed=6_000_000, transcendentals=0),
    )(
        tracers, u_courant, v_courant, w_courant, land_mask, weights,
        *(a.reshape(1, -1) for a in (src_block, dst_tile, dst_block, pattern)),
    )
    results = (new_tracers, fields, fluxes)
    return tuple(pl.pallas_call(
        deliver,
        out_shape=[jax.ShapeDtypeStruct(a.shape, a.dtype) for a in results],
        in_specs=[anywhere] * 3,
        out_specs=[anywhere] * 3,
        scratch_shapes=[pltpu.VMEM(a.shape, a.dtype) for a in results] + [dma((2 + ntr,)), dma((2 + ntr,))],
        compiler_params=pltpu.CompilerParams(vmem_limit_bytes=54 * 1024 * 1024),
    )(*results))


def solution(mesh):
    in_specs = (
        P(None, "lev", "tile", None),
        P("lev", "tile", None),
        P("lev", "tile", None),
        P("lev", "tile", None),
        P("tile", None),
        P(),
        P("tile"),
        P("tile", None),
        P("tile"),
        P("tile"),
    )
    out_specs = (P(None, "lev", "tile", None), P(None, "lev", "tile"), P(None, "lev", "tile"))
    return jax.shard_map(shards, mesh=mesh, in_specs=in_specs, out_specs=out_specs, check_vma=False)
```

```python
import jax
import jax.numpy as jnp
from jax import lax
from jax.experimental import pallas as pl
from jax.experimental.pallas import tpu as pltpu
from jax.sharding import PartitionSpec as P

MESH = pl.DeviceIdType.MESH
RING = 8
NBD = 16
GROUP = 16
BLOCKS = 24
SB = 512
DB = 256
PATTERNS = 8
SLOTS = 32
QUARTERS = (1, 2, 0, 3)
PARTS = 4
HALVES = (range(0, PARTS // 2), range(PARTS // 2, PARTS))


def minmod(first, second):
    return jnp.maximum(jnp.minimum(first, second), jnp.minimum(jnp.maximum(first, second), 0.0))


def coefficients(courant, opening):
    up, down = jnp.maximum(courant, 0.0) * opening, jnp.minimum(courant, 0.0) * opening
    return up, up * (0.5 * (1.0 - courant)), down, down * (0.5 * (1.0 + courant))


def flux(coefs, left, left_slope, right, right_slope):
    up, up_slope, down, down_slope = coefs
    return (up * left + up_slope * left_slope) + (down * right - down_slope * right_slope)


NEAR = {1: 1, 2: 3, 3: 5, 4: 7, 5: 6, 6: 4, 7: 2}


def slot_tables(tab_src, y, z, c, src_ref, tile_ref, block_ref, pattern_ref):
    entries = tile_ref.shape[1]
    targets = tile_ref[...]
    square = (entries, entries)
    row_i = lax.broadcasted_iota(jnp.int32, square, 0)
    lane_i = lax.broadcasted_iota(jnp.int32, square, 1)
    as_rows = jnp.broadcast_to(targets.astype(jnp.float32), square)
    same = jnp.where((jnp.transpose(as_rows) == as_rows) & (row_i < lane_i), 1.0, 0.0)
    rank = jnp.sum(same, axis=0, keepdims=True).astype(jnp.int32)
    ty, tz, tc = targets >> 4, (targets >> 1) & 7, targets & 1
    low = jnp.bitwise_xor(tc, c) * 2 + rank
    value, slot_i = row_i // SLOTS, lax.rem(row_i, SLOTS)
    named = jnp.where(value == 0, src_ref[...] + 1, jnp.where(value == 1, pattern_ref[...] + 1, block_ref[...] + 1))
    named = jnp.where(value == 3, 0, named).astype(jnp.float32)
    place_i = lax.broadcasted_iota(jnp.int32, (16, entries), 0)
    for h, place, slot in ((0, tz, ((ty - y) & 7) * 4 + low), (1, ty, ((tz - z) & 7) * 4 + low)):
        filled = jnp.where(slot == slot_i, named, 0.0).astype(jnp.bfloat16)
        chosen = jnp.where(place == place_i, 1.0, 0.0).astype(jnp.bfloat16)
        table = lax.dot_general(chosen, filled, (((1,), (1,)), ((), ())), preferred_element_type=jnp.float32)
        table = table.astype(jnp.int32) - 1
        for p in range(8):
            tab_src[h * 8 + p] = jnp.broadcast_to(table[p : p + 1, :], (8, 128))


def kernel(
    tr_hbm, u_hbm, v_hbm, w_hbm, land_hbm, weights_hbm, src_ref, tile_ref, block_ref, pattern_ref,
    new_hbm, out0, out1,
    tr, u_ref, v_ref, w_ref, land_ref, weights,
    up_out, down_out, up_in, down_in, w_in, east_out, west_out, west_in, east_in,
    fold_out, fold_in, mirrored, tab_src, tab_in, tab, tab_s, div, staged, new_ref,
    x_ref, ag, prod, terms, terms_out, masks, acc, rs_out, rs_in,
    load, send, recv, ag_send, ag_recv, sib_send, sib_recv, rs_send, rs_recv,
):
    tiles, levs = lax.axis_size("tile"), lax.axis_size("lev")
    me, lev = lax.axis_index("tile"), lax.axis_index("lev")
    y, z, c = me // 16, lax.rem(me // 2, 8), lax.rem(me, 2)
    ntr, nlev, cols, rows = tr.shape

    def strip(yy, zz, cc):
        return {"tile": yy * 16 + zz * 2 + cc}

    east, west = {"tile": lax.rem(me + 1, tiles)}, {"tile": lax.rem(me + tiles - 1, tiles)}
    fold = {"tile": tiles - 1 - me}
    below, above = {"lev": lax.rem(lev + 1, levs)}, {"lev": lax.rem(lev + levs - 1, levs)}
    sibling = strip(y, z, 1 - c)
    table_to = []
    for o in range(1, 8):
        zz, yy = lax.rem(z + o, 8), lax.rem(y + o, 8)
        table_to.append((o, 0, zz, strip(y, zz, c)))
        table_to.append((o, 1, yy, strip(yy, z, c)))
    partners = [east, west, fold, below, above] + [entry[3] for entry in table_to]
    along_z = (strip(y, lax.rem(z + 1, RING), c), strip(y, lax.rem(z + RING - 1, RING), c))
    along_y = (strip(lax.rem(y + 1, RING), z, c), strip(lax.rem(y + RING - 1, RING), z, c))
    gather_to = (along_z, along_y)
    reduce_to = (along_y, along_z)

    barrier = pltpu.get_barrier_semaphore()
    for other in partners:
        pl.semaphore_signal(barrier, inc=1, device_id=other, device_id_type=MESH)
    loads = [
        pltpu.make_async_copy(src, dst, load.at[n])
        for n, (src, dst) in enumerate((
            (tr_hbm, tr), (land_hbm, land_ref), (v_hbm, v_ref), (u_hbm, u_ref), (w_hbm, w_ref), (weights_hbm, weights)
        ))
    ]
    for copy in loads[:5]:
        copy.start()
    slot_tables(tab_src, y, z, c, src_ref, tile_ref, block_ref, pattern_ref)
    loads[0].wait()
    def cast(n):
        for t in range(ntr):
            for out, k in ((down_out, 0), (up_out, nlev - 2)):
                two = [tr[t, k + m, n * 8 : n * 8 + 8, :] for m in range(2)]
                out[n, t * 16 : t * 16 + 16, :] = jnp.concatenate(two, 0).astype(jnp.bfloat16)

    cast(QUARTERS[0])
    loads[4].wait()
    pl.semaphore_wait(barrier, len(partners))

    copies = []
    started = []

    def start(copy):
        copy.start()
        started.append(copy)

    def send_to(src, dst, other):
        n = len(copies)
        copies.append(pltpu.make_async_remote_copy(
            src_ref=src, dst_ref=dst, send_sem=send.at[n], recv_sem=recv.at[n], device_id=other, device_id_type=MESH,
        ))
        start(copies[-1])
        return copies[-1]

    def send_levels(n):
        at = pl.ds(n * 8, 8)
        return [
            send_to(up_out.at[n], up_in.at[n], below),
            send_to(down_out.at[n], down_in.at[n], above),
            send_to(w_ref.at[nlev - 1, at], w_in.at[at], below),
        ]

    sent_lev = {QUARTERS[0]: send_levels(QUARTERS[0])}
    for n in range(1, 4):
        loads[n].wait()
    lane = lax.broadcasted_iota(jnp.int32, (cols, 128), 1)
    top = rows - 128
    packed = jnp.zeros((cols, 128), jnp.float32)
    for q in range(ntr * nlev):
        tile = tr[q // nlev, q % nlev, :, top:]
        packed = jnp.where(lane == 2 * q, pltpu.roll(tile, (2 * q + 1) % 128, 1), packed)
        packed = jnp.where(lane == 2 * q + 1, pltpu.roll(tile, (2 * q + 3) % 128, 1), packed)
    first = 2 * ntr * nlev
    for k in range(nlev):
        packed = jnp.where(lane == first + k, pltpu.roll(v_ref[k, :, top:], first + k + 1, 1), packed)
    ocean = land_ref[...].astype(jnp.float32)
    packed = jnp.where(lane == first + nlev, pltpu.roll(ocean[:, top:], first + nlev + 1, 1), packed)
    fold_out[...] = packed
    sent_fold = [send_to(fold_out, fold_in, fold)]
    for n in QUARTERS[1:]:
        cast(n)
        sent_lev[n] = send_levels(n)
    last = cols - 8
    east_out[first : first + 8, :] = jnp.zeros((8, rows), jnp.float32)
    west_out[first : first + 8, :] = jnp.zeros((8, rows), jnp.float32)
    for q in range(ntr * nlev):
        east_out[2 * q : 2 * q + 2, :] = tr[q // nlev, q % nlev, cols - 2 : cols, :]
        west_out[2 * q : 2 * q + 2, :] = tr[q // nlev, q % nlev, 0:2, :]
    for k in range(nlev):
        east_out[first + k : first + k + 1, :] = u_ref[k, cols - 1 : cols, :]
    east_out[first + nlev : first + nlev + 1, :] = ocean[cols - 1 : cols]
    west_out[first + nlev : first + nlev + 1, :] = ocean[0:1]
    sent_side = [send_to(east_out, west_in, east), send_to(west_out, east_in, west)]
    sent_table = [
        send_to(tab_src.at[h * 8 + row], tab_in.at[h * 8 + NEAR[o]], other) for o, h, row, other in table_to
    ]

    loads[5].start()

    def ahead(a, axis):
        return pltpu.roll(a, a.shape[axis] - 1, axis)

    def behind(a, axis):
        return pltpu.roll(a, 1, axis)

    def east_part(cells, courants, mask, columns, at):
        opening = mask * ahead(mask, 0)
        for k in range(nlev):
            coefs = coefficients(courants(k), opening)
            for t in range(ntr):
                x = cells(t, k)
                beyond = ahead(x, 0)
                step = beyond - x
                slope = minmod(behind(step, 0), step)
                out = flux(coefs, x, slope, beyond, ahead(slope, 0))
                div[t, k, columns, :] = (out - behind(out, 0))[at]

    inner = slice(8, cols - 8)
    east_part(lambda t, k: tr[t, k], lambda k: u_ref[k], ocean, inner, inner)

    def unpacked(packed_ref, row, at):
        tile = packed_ref[row // 8 * 8 : row // 8 * 8 + 8, :]
        turn = (at - row) % 8
        return pltpu.roll(tile, turn, 0) if turn else tile

    def east_ends(n):
        if n == 0:
            mask = jnp.concatenate([unpacked(west_in, first + nlev, 7), ocean[:16]], 0)
            east_part(
                lambda t, k: jnp.concatenate([unpacked(west_in, 2 * (t * nlev + k), 6), tr[t, k, :16, :]], 0),
                lambda k: jnp.concatenate([unpacked(west_in, first + k, 7), u_ref[k, :16, :]], 0),
                mask, slice(0, 8), slice(8, 16),
            )
        else:
            mask = jnp.concatenate([ocean[cols - 16 :], unpacked(east_in, first + nlev, 0)], 0)
            east_part(
                lambda t, k: jnp.concatenate([tr[t, k, cols - 16 :, :], unpacked(east_in, 2 * (t * nlev + k), 0)], 0),
                lambda k: jnp.concatenate([u_ref[k, cols - 16 :, :], jnp.zeros((8, rows), jnp.float32)], 0),
                mask, slice(last, cols), slice(8, 16),
            )

    for copy in sent_fold:
        copy.wait_recv()
    for i in range(cols):
        mirrored[cols - 1 - i : cols - i, :] = fold_in[i : i + 1, :]
    ghosts = mirrored[...]
    nothing = jnp.zeros((cols, 128), jnp.float32)
    ocean_wide = jnp.concatenate(
        [ocean, jnp.where(lane == 0, pltpu.roll(ghosts, 128 - first - nlev, 1), 0.0)], 1
    )
    open_north = ocean_wide * ahead(ocean_wide, 1)

    def north_part(part):
        for k in range(nlev):
            v = v_ref[k, part, :]
            other = pltpu.roll(ghosts[part], (127 - first - k) % 128, 1)
            fixed = jnp.where(lane[part] == 127, 0.5 * (v[:, top:] - other), v[:, top:])
            courant = jnp.concatenate([v[:, :top], fixed, nothing[part]], 1)
            coefs = coefficients(courant, open_north[part])
            for t in range(ntr):
                ghost = pltpu.roll(ghosts[part], (128 - 2 * (t * nlev + k)) % 128, 1)
                x = jnp.concatenate([tr[t, k, part, :], jnp.where(lane[part] < 2, ghost, 0.0)], 1)
                beyond = ahead(x, 1)
                step = beyond - x
                slope = minmod(behind(step, 1), step)
                north = flux(coefs, x, slope, beyond, ahead(slope, 1))
                div[t, k, part, :] += (north - behind(north, 1))[:, :rows]

    streams = [(h, d) for h in range(2) for d in range(2)]
    quarter = BLOCKS // 4

    def gather_copy(h, d, n):
        k, at = (n // 4 + 1, n % 4) if n < 12 else (4, 2 * (n - 12) + d)
        blocks = pl.ds(quarter * at, quarter)
        src = x_ref.at[h, pl.ds(quarter * QUARTERS[at], quarter)] if k == 1 else ag.at[h, d, k - 2, blocks]
        dst = ag.at[h, 0 if k == 4 else d, k - 1, blocks]
        return pltpu.make_async_remote_copy(
            src_ref=src, dst_ref=dst, send_sem=ag_send.at[h, d, n], recv_sem=ag_recv.at[h, d, n],
            device_id=gather_to[h][d], device_id_type=MESH,
        )

    not_first = jnp.where(lev > 0, 1.0, 0.0).astype(jnp.float32)
    not_last = jnp.where(lev < levs - 1, 1.0, 0.0).astype(jnp.float32)
    across = rows // 128
    for turn, quarter_at in enumerate(QUARTERS):
        i0 = quarter_at * 8
        part = slice(i0, i0 + 8)
        if turn == 2:
            for copy in sent_side:
                copy.wait_recv()
        if turn >= 2:
            east_ends(quarter_at)
        north_part(part)
        for copy in sent_lev[quarter_at]:
            copy.wait_recv()
        open_part = land_ref[part, :].astype(jnp.float32)
        coefs = [coefficients(w_in[part, :], open_part * not_first)]
        for k in range(nlev):
            coefs.append(coefficients(w_ref[k, part, :], open_part * not_last if k == nlev - 1 else open_part))
        for t in range(ntr):
            beneath, over = (a[quarter_at, t * 16 : t * 16 + 16, :].astype(jnp.float32) for a in (down_in, up_in))
            cells = [over[:8] * not_first, over[8:] * not_first]
            cells += [tr[t, k, part, :] for k in range(nlev)]
            cells += [beneath[:8] * not_last, beneath[8:] * not_last]
            steps = [b - a for a, b in zip(cells[:-1], cells[1:])]
            slopes = [minmod(a, b) for a, b in zip(steps[:-1], steps[1:])]
            faces = [
                flux(coefs[f], cells[f + 1], slopes[f], cells[f + 2], slopes[f + 1]) for f in range(nlev + 1)
            ]
            for k in range(nlev):
                total = div[t, k, part, :] + (faces[k + 1] - faces[k])
                new = cells[k + 2] - total
                new_ref[t, k, part, :] = new
                q = t * nlev + k
                for kind, value in ((0, new), (1, total)):
                    for m in range(across):
                        at = (i0 * across + m) * GROUP + q
                        staged[kind, pl.ds(at, 8, stride=GROUP * across), :] = value[:, m * 128 : m * 128 + 128]
        for kind in range(2):
            for b in range(i0 * rows // SB, (i0 + 8) * rows // SB):
                for m in range(SB // 128):
                    at = (b * (SB // 128) + m) * GROUP
                    x_ref[kind, b, :, m * 128 : m * 128 + 128] = staged[kind, at : at + GROUP, :].astype(jnp.bfloat16)
        for h, d in streams:
            start(gather_copy(h, d, turn))
    new_copy = pltpu.make_async_copy(new_ref, new_hbm, load.at[7])
    new_copy.start()

    lanes = 2 * 8 * 2 * GROUP
    sub_i = lax.broadcasted_iota(jnp.int32, (NBD * GROUP, lanes), 0)
    lane_i = lax.broadcasted_iota(jnp.int32, (NBD * GROUP, lanes), 1)
    wanted = jnp.where(lax.rem(sub_i, GROUP) == lax.rem(lane_i, GROUP), sub_i // GROUP, -2)
    slot_of_lane = lax.broadcasted_iota(jnp.int32, (1, lanes), 1) // GROUP

    def one_mask(i, carry):
        h, q = i // 8, lax.rem(i, 8)
        blocks = jnp.full((1, lanes), -1, jnp.int32)
        for core in range(2):
            for j in range(8):
                for r in range(2):
                    named = tab_s[core * 16 + h * 8 + j, 2 * SLOTS + q * 4 + core * 2 + r]
                    blocks = jnp.where(slot_of_lane == (core * 8 + j) * 2 + r, named, blocks)
        masks[i] = jnp.where(blocks == wanted, 1.0, 0.0).astype(jnp.bfloat16)
        return carry


    def sibling_copy(h, j):
        at = pl.ds((8 + j) * 2 * GROUP, 2 * GROUP)
        return pltpu.make_async_remote_copy(
            src_ref=terms_out.at[h, j], dst_ref=terms.at[pl.ds(h * 8, 8), at],
            send_sem=sib_send.at[h, j], recv_sem=sib_recv.at[h, j], device_id=sibling, device_id_type=MESH,
        )

    def multiply(at, view, first_quarter, places):
        count = quarter * len(places)
        x = view[quarter * first_quarter : quarter * first_quarter + count].reshape(count * GROUP, SB)

        def one_pattern(p, carry):
            r = jnp.dot(x, weights[p], preferred_element_type=jnp.float32)
            r = r.astype(jnp.bfloat16).reshape(count, GROUP, DB)
            for i, place in enumerate(places):
                prod[at, pl.ds(p * BLOCKS + quarter * place, quarter)] = r[i * quarter : (i + 1) * quarter]
            return carry

        lax.fori_loop(0, PATTERNS, one_pattern, 0, unroll=PATTERNS)

    def pick(h, j, at):
        def product(slot):
            src, pat = tab_s[h * 8 + j, slot], tab_s[h * 8 + j, SLOTS + slot]
            return prod[at, jnp.clip(pat * BLOCKS + src, 0, PATTERNS * BLOCKS - 1)]

        def one_target(q, carry):
            for r in range(2):
                terms_out[h, j, q, r * GROUP : (r + 1) * GROUP, :] = product(q * 4 + 2 + r)
            for r in range(2):
                at = (j * 2 + r) * GROUP
                terms[h * 8 + q, at : at + GROUP, :] = product(q * 4 + r)
            return carry

        lax.fori_loop(0, 8, one_target, 0, unroll=4)
        start(sibling_copy(h, j))

    def own(h):
        multiply(h * 2, x_ref.at[h], 0, range(4))
        pick(h, 0, h * 2)

    def whole(k, h, d):
        multiply(h * 2 + d, ag.at[h, d, k - 1], 0, QUARTERS)
        pick(h, 2 * k - 1 + d, h * 2 + d)

    def early(k, h, d):
        multiply(h * 2 + d, ag.at[h, d, k - 1], 0, QUARTERS[:2])

    def late(k, h, d):
        multiply(h * 2 + d, ag.at[h, d, k - 1], 2, QUARTERS[2:])
        pick(h, 2 * k - 1 + d, h * 2 + d)

    waiting = [(own, 0), (own, 1)]
    todo = {3: (whole, 1), 5: (early, 2), 7: (late, 2), 9: (early, 3), 11: (late, 3)}
    for n in range(12):
        for h, d in streams:
            gather_copy(h, d, n).wait_recv()
            if n < 8:
                start(gather_copy(h, d, n + 4))
            elif n % 2 == d:
                start(gather_copy(h, d, 12 + (n - 8) // 2))
        if n == 0:
            for copy in sent_table:
                copy.wait_recv()
            for h, row in ((0, z), (1, y)):
                tab[h * 8 : h * 8 + 1, :] = tab_src[h * 8 + row, 0:1, :]
                for j in range(1, 8):
                    tab[h * 8 + j : h * 8 + j + 1, :] = tab_in[h * 8 + j, 0:1, :]
            sent_tables = send_to(tab.at[pl.ds(0, 16)], tab.at[pl.ds(16, 16)], sibling)

        elif n == 1:
            sent_tables.wait_recv()
            to_scalars = pltpu.make_async_copy(tab, tab_s, load.at[6])
            to_scalars.start()
            to_scalars.wait()
            lax.fori_loop(0, 16, one_mask, 0)
            loads[5].wait()
        for _ in range(2 if n > 1 else 0):
            if waiting:
                work, *of = waiting.pop(0)
                work(*of)
        if n in todo:
            waiting += [(*todo[n], h, d) for h, d in streams]
    for work, *of in waiting:
        work(*of)
    for n, work in ((12, early), (13, late)):
        for h in range(2):
            for d in range(2):
                gather_copy(h, d, n).wait_recv()
            work(4, h, 0)

    size = NBD * GROUP // PARTS

    def partial(h, *targets):
        for q in targets:
            acc[h, q] = jnp.dot(masks[h * 8 + q], terms[h * 8 + q], preferred_element_type=jnp.float32)

    def reduce_copy(h, d, s, part):
        at = pl.ds(part * size, size)
        n = PARTS * s + part
        return pltpu.make_async_remote_copy(
            src_ref=rs_out.at[h, d, s, at], dst_ref=rs_in.at[h, d, s, at],
            send_sem=rs_send.at[h, d, n], recv_sem=rs_recv.at[h, d, n],
            device_id=reduce_to[h][d], device_id_type=MESH,
        )

    def came(h, d, s, part, at):
        reduce_copy(h, d, s, part).wait_recv()
        return rs_in[h, d, s, at].astype(jnp.float32)

    def pass_on(h, d, s, part):
        at = pl.ds(part * size, size)
        total = acc[h, 4 - s if d == 0 else 4 + s, at]
        if s > 1 or (s == 1 and part in HALVES[d]):
            total += came(h, d, s - 1, part, at)
        rs_out[h, d, s, at] = total.astype(jnp.bfloat16)
        start(reduce_copy(h, d, s, part))

    order = [[*HALVES[1 - d], *HALVES[d]] for d in range(2)]
    for h in range(2):
        for j in range(8):
            sibling_copy(h, j).wait_recv()
        partial(h, 4)
        for p in range(PARTS // 2):
            for d in range(2):
                pass_on(h, d, 0, HALVES[d][p])
    for h in range(2):
        partial(h, 3, 5)
        for p in range(PARTS // 2):
            for d in range(2):
                pass_on(h, d, 1, order[d][p])
    for h in range(2):
        partial(h, 2, 6)
    for p in range(PARTS // 2, PARTS):
        for h, d in streams:
            pass_on(h, d, 1, order[d][p])
    for h in range(2):
        partial(h, 1, 7)
    for p in range(PARTS):
        for h, d in streams:
            pass_on(h, d, 2, order[d][p])
    for h in range(2):
        partial(h, 0)
    for p in range(PARTS):
        for h, d in streams:
            pass_on(h, d, 3, order[d][p])
    for p in range(PARTS):
        for h, out in ((0, out0), (1, out1)):
            part = order[0][p]
            at = pl.ds(part * size, size)
            total = acc[h, 0, at] + came(h, 0, 3, part, at) + came(h, 1, 3, part, at)
            for i in range(size // GROUP):
                b = part * (size // GROUP) + i
                for t in range(ntr):
                    at_row = i * GROUP + t * nlev
                    out[t, :, b * DB : (b + 1) * DB] = total[at_row : at_row + nlev]
    new_copy.wait()
    for copy in started:
        copy.wait_send()


def deliver(new_in, fields_in, fluxes_in, new_out, fields_out, fluxes_out, new, fields, fluxes, load, store):
    pieces = [(fields_in, fields, fields_out), (fluxes_in, fluxes, fluxes_out)]
    pieces += [(new_in.at[t], new.at[t], new_out.at[t]) for t in range(new.shape[0])]
    loads = [pltpu.make_async_copy(src, held, load.at[n]) for n, (src, held, _) in enumerate(pieces)]
    stores = [pltpu.make_async_copy(held, dst, store.at[n]) for n, (_, held, dst) in enumerate(pieces)]
    for copy in loads:
        copy.start()
    for arriving, leaving in zip(loads, stores):
        arriving.wait()
        leaving.start()
    for copy in stores:
        copy.wait()


def shards(
    tracers,
    u_courant,
    v_courant,
    w_courant,
    land_mask,
    weights,
    src_block,
    dst_tile,
    dst_block,
    pattern,
):
    vmem = pl.BlockSpec(memory_space=pltpu.VMEM)
    anywhere = pl.BlockSpec(memory_space=pl.ANY)
    f32, bf16, i32 = jnp.float32, jnp.bfloat16, jnp.int32
    ntr, nlev, cols, rows = tracers.shape
    height = NBD * GROUP
    dma = pltpu.SemaphoreType.DMA
    messages = 1 + 2 + 12 + 14 + 1
    new_tracers, fields, fluxes = pl.pallas_call(
        kernel,
        out_shape=[
            jax.ShapeDtypeStruct(tracers.shape, f32),
            jax.ShapeDtypeStruct((ntr, nlev, NBD * DB), f32),
            jax.ShapeDtypeStruct((ntr, nlev, NBD * DB), f32),
        ],
        in_specs=[anywhere] * 6 + [vmem] * 4,
        out_specs=[anywhere, vmem, vmem],
        scratch_shapes=[
            pltpu.VMEM(tracers.shape, f32),
            pltpu.VMEM((nlev, cols, rows), f32),
            pltpu.VMEM((nlev, cols, rows), f32),
            pltpu.VMEM((nlev, cols, rows), f32),
            pltpu.VMEM((cols, rows), i32),
            pltpu.VMEM(weights.shape, bf16),
            pltpu.VMEM((4, ntr * 16, rows), bf16),
            pltpu.VMEM((4, ntr * 16, rows), bf16),
            pltpu.VMEM((4, ntr * 16, rows), bf16),
            pltpu.VMEM((4, ntr * 16, rows), bf16),
            pltpu.VMEM((cols, rows), f32),
            pltpu.VMEM((2 * ntr * nlev + 8, rows), f32),
            pltpu.VMEM((2 * ntr * nlev + 8, rows), f32),
            pltpu.VMEM((2 * ntr * nlev + 8, rows), f32),
            pltpu.VMEM((2 * ntr * nlev + 8, rows), f32),
            pltpu.VMEM((cols, 128), f32),
            pltpu.VMEM((cols, 128), f32),
            pltpu.VMEM((cols, 128), f32),
            pltpu.VMEM((16, 8, 128), i32),
            pltpu.VMEM((16, 8, 128), i32),
            pltpu.VMEM((32, 128), i32),
            pltpu.SMEM((32, 128), i32),
            pltpu.VMEM(tracers.shape, f32),
            pltpu.VMEM((2, BLOCKS * SB // 128 * GROUP, 128), f32),
            pltpu.VMEM(tracers.shape, f32),
            pltpu.VMEM((2, BLOCKS, GROUP, SB), bf16),
            pltpu.VMEM((2, 2, 4, BLOCKS, GROUP, SB), bf16),
            pltpu.VMEM((4, PATTERNS * BLOCKS, GROUP, DB), bf16),
            pltpu.VMEM((16, 32 * GROUP, DB), bf16),
            pltpu.VMEM((2, 8, 8, 2 * GROUP, DB), bf16),
            pltpu.VMEM((16, height, 32 * GROUP), bf16),
            pltpu.VMEM((2, RING, height, DB), f32),
            pltpu.VMEM((2, 2, 4, height, DB), bf16),
            pltpu.VMEM((2, 2, 4, height, DB), bf16),
            dma((8,)),
            dma((messages,)),
            dma((messages,)),
            dma((2, 2, 14)),
            dma((2, 2, 14)),
            dma((2, 8)),
            dma((2, 8)),
            dma((2, 2, 4 * PARTS)),
            dma((2, 2, 4 * PARTS)),
        ],
        compiler_params=pltpu.CompilerParams(
            collective_id=1, has_side_effects=True, vmem_limit_bytes=54 * 1024 * 1024
        ),
        cost_estimate=pl.CostEstimate(flops=14_000_000_000, bytes_accessed=6_000_000, transcendentals=0),
    )(
        tracers, u_courant, v_courant, w_courant, land_mask, weights,
        *(a.reshape(1, -1) for a in (src_block, dst_tile, dst_block, pattern)),
    )
    results = (new_tracers, fields, fluxes)
    return tuple(pl.pallas_call(
        deliver,
        out_shape=[jax.ShapeDtypeStruct(a.shape, a.dtype) for a in results],
        in_specs=[anywhere] * 3,
        out_specs=[anywhere] * 3,
        scratch_shapes=[pltpu.VMEM(a.shape, a.dtype) for a in results] + [dma((2 + ntr,)), dma((2 + ntr,))],
        compiler_params=pltpu.CompilerParams(vmem_limit_bytes=54 * 1024 * 1024),
    )(*results))


def solution(mesh):
    in_specs = (
        P(None, "lev", "tile", None),
        P("lev", "tile", None),
        P("lev", "tile", None),
        P("lev", "tile", None),
        P("tile", None),
        P(),
        P("tile"),
        P("tile", None),
        P("tile"),
        P("tile"),
    )
    out_specs = (P(None, "lev", "tile", None), P(None, "lev", "tile"), P(None, "lev", "tile"))
    return jax.shard_map(shards, mesh=mesh, in_specs=in_specs, out_specs=out_specs, check_vma=False)
```
